32 devices in a mesh: groups: 2 (over x), expert: 16 (over z, y, core).
Axes of the slice: x: 2, y: 2, z: 4, core: 2. Of those that a mesh axis runs over, the one named last changes fastest.
Arguments:
- prefill_tokens: bfloat16 [1024, 7168], P(('groups', 'expert')), parts along dimension 0, may hold values from -6 to 6
- prefill_experts: int32 [1024, 8], P(('groups', 'expert')), parts along dimension 0, may hold values from 0 to 7, as said below
- prefill_gates: int32 [1024, 8], P(('groups', 'expert')), parts along dimension 0, may hold values from 2048 to 65536
- decode_rows: bfloat16 [1024, 7168], P(('groups', 'expert')), parts along dimension 0, may hold values from -6 to 6
- decode_experts: int32 [1024, 8], P(('groups', 'expert')), parts along dimension 0, may hold values from 0 to 7, as said below
- decode_gates: int32 [1024, 8], P(('groups', 'expert')), parts along dimension 0, may hold values from 2048 to 65536
- w_gate_up: bfloat16 [16, 7168, 1024], P('expert'), may hold values from -0.0625 to 0.0625
- w_down: bfloat16 [16, 512, 7168], P('expert'), may hold values from -0.1875 to 0.1875
- queries: bfloat16 [1024, 64, 576], P(('groups', 'expert')), parts along dimension 0, may hold values from -21 to 21
- own_latent: bfloat16 [1024, 576], P(('groups', 'expert')), parts along dimension 0, may hold values from -6 to 6
- latents: bfloat16 [512, 64, 576], P(('groups', 'expert')), parts along dimension 0, may hold values from -6 to 6
- span_owner: int32 [512], P(('groups', 'expert')), parts along dimension 0, may hold values from 0 to 15, as said below
- span_request: int32 [512], P(('groups', 'expert')), parts along dimension 0, may hold values from 0 to 31
- span_length: int32 [512], P(('groups', 'expert')), parts along dimension 0, may hold values from 1 to 64
Outputs:
- prefill_out: bfloat16 [1024, 7168], P(('groups', 'expert')), parts along dimension 0
- decode_out: bfloat16 [1024, 7168], P(('groups', 'expert')), parts along dimension 0
- context: bfloat16 [1024, 64, 512], P(('groups', 'expert')), parts along dimension 0
The draws below stay inside these ranges and needn't reach their ends.
There are 2 independent parts, one for each index of `groups`. The reference program is written for one: setup_inputs(seed, part) draws one part's arguments, and reference() takes and returns one part's arrays. A program takes and returns all parts, laid end to end along the dimension named above; an argument that names none is the same for every part. Nothing has to cross between parts.
Inputs may be any that keep to these rules, and one draw needn't show every extreme that they name: `prefill_experts`: the 8 experts of a row differ. One expert, drawn from the seed and the same for the decode rows, is named by every row; among the rows of one device no expert is named more than 32 times, and the other experts share the remaining picks of that device evenly. `decode_experts`: the 8 experts of a row differ. One expert, drawn from the seed and the same for the prefill tokens, is named by every row; among the rows of one device no expert is named more than 32 times, and the other experts share the remaining picks of that device evenly. `span_owner`: of the blocks of one device, either none or exactly 2 have the same owner; a few owners, drawn from the seed, receive 2 blocks from every device.
All inputs are finite; a program needn't handle non-finite values.
Results may differ from the reference program's by a relative error of at most 0.008.
Values may be sent and summed in bfloat16 or wider, within the bound.
No kernel may reach another device: no remote copies, remote signals or barrier semaphores. Data moves between devices by JAX's collectives and lax.ppermute only.
A program may use at most 256 MiB of HBM per device.

```python
import jax
import jax.numpy as jnp
from jax import lax

D = 7168
HID = 1024
H_DEV = 512
TOP = 8
KV = 512
LAT = 576
HEADS = 64
BLK = 64
CAPC = 2
P_DEV = 32
R_DEV = 32
CH_DEV = 16
EXPERTS = 8
SLICES = 16
DECODE_OWNERS = 16
PRE_TOKENS = 512
DEC_ROWS = 512
SPANS = 256


def hot_expert(key):
    return jax.random.randint(jax.random.fold_in(key, 11), (), 0, EXPERTS)


def routed_ids(key, hot_choice, per_device, block_list):
    others = EXPERTS - 1
    first_key, second_key, third_key = jax.random.split(key, 3)
    shuffles = jax.vmap(lambda single: jax.random.permutation(single, others))(jax.random.split(first_key, block_list))
    offsets = jax.random.randint(second_key, (block_list,), 0, others)
    places = (offsets[:, None, None] + jnp.arange(per_device)[None, :, None] * (TOP - 1) + jnp.arange(TOP - 1)[None, None, :]) % others
    chosen = shuffles[jnp.arange(block_list)[:, None, None], places].astype(jnp.int32)
    chosen = chosen + (chosen >= hot_choice).astype(jnp.int32)
    together = jnp.concatenate([jnp.broadcast_to(hot_choice, (block_list, per_device, 1)).astype(jnp.int32), chosen], axis=2)
    sorting = jax.random.randint(third_key, (block_list, per_device, TOP), 0, 1 << 20) * TOP + jnp.arange(TOP)[None, None, :]
    arrangement = jnp.argsort(sorting, axis=2)
    result = jnp.take_along_axis(together, arrangement, axis=2)
    return result.reshape(block_list * per_device, TOP).astype(jnp.int32)


def draw_prefill_experts(key, part):
    hot_choice = hot_expert(key)
    key = jax.random.fold_in(key, 21)
    return routed_ids(key, hot_choice, P_DEV, PRE_TOKENS // P_DEV)


def draw_decode_experts(key, part):
    hot_choice = hot_expert(key)
    key = jax.random.fold_in(key, 22)
    return routed_ids(key, hot_choice, R_DEV, DEC_ROWS // R_DEV)


def span_plan(key):
    inner_key = jax.random.fold_in(key, 31)
    owner_key, score_random_key, order_key, request_key = jax.random.split(inner_key, 4)
    block_list = SPANS // CH_DEV
    popular_expert_count = min(4, CH_DEV // CAPC)
    expert_ranking = jax.random.permutation(owner_key, DECODE_OWNERS)
    extra_score_boost = jnp.where(expert_ranking < popular_expert_count, 1 << 13, 0)
    expert_scores = (jax.random.randint(score_random_key, (block_list, DECODE_OWNERS), 0, 1 << 12) + extra_score_boost[None, :]) * DECODE_OWNERS + jnp.arange(DECODE_OWNERS)[None, :]
    unused_values, chosen = lax.top_k(expert_scores.astype(jnp.int32), CH_DEV // CAPC)
    owners = jnp.repeat(chosen, CAPC, axis=1)
    sorting = jax.random.randint(order_key, (block_list, CH_DEV), 0, 1 << 20) * CH_DEV + jnp.arange(CH_DEV)[None, :]
    owners = jnp.take_along_axis(owners, jnp.argsort(sorting, axis=1), axis=1)
    requests = jax.random.randint(request_key, (block_list, CH_DEV), 0, R_DEV)
    return (owners.reshape(-1).astype(jnp.int32), requests.reshape(-1).astype(jnp.int32))


def draw_span_owner(key, part):
    owners, requests = span_plan(key)
    return owners


def draw_span_request(key, part):
    owners, requests = span_plan(key)
    return requests


def draw_queries(key, part):
    key = jax.random.fold_in(key, 51)
    values = jax.random.truncated_normal(key, -6.0, 6.0, (DEC_ROWS, HEADS, LAT), jnp.float32)
    return values.astype(jnp.bfloat16)


def draw_own_latent(key, part):
    key = jax.random.fold_in(key, 61)
    values = jax.random.truncated_normal(key, -6.0, 6.0, (DEC_ROWS, LAT), jnp.float32)
    return values.astype(jnp.bfloat16)


def draw_latents(key, part):
    key = jax.random.fold_in(key, 71)
    values = jax.random.truncated_normal(key, -6.0, 6.0, (SPANS, BLK, LAT), jnp.float32)
    return values.astype(jnp.bfloat16)


def plant(drawn, stream_key, least, largest):
    extent = drawn.shape
    index_at = [jax.random.randint(jax.random.fold_in(stream_key, axis), (), 0, extent[axis]) for axis in range(len(extent))]
    drawn = drawn.at[tuple(index_at)].set(least)
    longest = extent.index(max(extent))
    index_at[longest] = (index_at[longest] + 1) % extent[longest]
    return drawn.at[tuple(index_at)].set(largest)


def shard_levels(stream_key, shape, cuts, least, top_value):
    def one(axis_at, shards_of):
        draws = jax.random.uniform(jax.random.fold_in(jax.random.fold_in(stream_key, 6), axis_at), (shards_of,), jnp.float32, least / len(cuts), top_value / len(cuts))
        return jnp.repeat(jnp.exp(draws), shape[axis_at] // shards_of).reshape((-1,) + (1,) * (len(shape) - axis_at - 1))

    level = one(*cuts[0])
    for cut in cuts[1:]:
        level = level * one(*cut)
    return level


def scatter_about(own_key, shape, spread, reach, cuts=(), held_as=jnp.bfloat16):
    entries = jax.random.normal(own_key, shape, jnp.float32) * spread
    if len(cuts) > 0:
        entries = shard_levels(own_key, shape, cuts, -0.22, 0.18) * entries
    return jnp.clip(entries, min=-reach, max=reach).astype(held_as)


def setup_inputs(seed: int = 0, part: int = 0) -> dict:
    keys = jax.random.split(jax.random.key(seed), 15)
    part_keys = jax.random.split(jax.random.fold_in(keys[14], part), 15)
    return {
        "prefill_tokens": scatter_about(part_keys[0], (PRE_TOKENS, D), 1.0, 6.0, ((0, 16),)),
        "prefill_experts": draw_prefill_experts(jax.random.fold_in(jax.random.fold_in(keys[14], part), 71), part),
        "prefill_gates": plant(jax.random.randint(part_keys[2], (PRE_TOKENS, TOP), 2048, 65537), jax.random.fold_in(part_keys[2], 1), 2048, 65536).astype(jnp.int32),
        "decode_rows": scatter_about(part_keys[3], (DEC_ROWS, D), 1.0, 6.0, ((0, 16),)),
        "decode_experts": draw_decode_experts(jax.random.fold_in(jax.random.fold_in(keys[14], part), 71), part),
        "decode_gates": plant(jax.random.randint(part_keys[5], (DEC_ROWS, TOP), 2048, 65537), jax.random.fold_in(part_keys[5], 1), 2048, 65536).astype(jnp.int32),
        "w_gate_up": scatter_about(keys[6], (SLICES, D, 2 * H_DEV), D ** -0.5, 0.0625, ((0, 16),)),
        "w_down": scatter_about(keys[7], (SLICES, H_DEV, D), HID ** -0.5, 0.1875, ((0, 16),)),
        "queries": draw_queries(jax.random.fold_in(jax.random.fold_in(keys[14], part), 71), part),
        "own_latent": draw_own_latent(jax.random.fold_in(jax.random.fold_in(keys[14], part), 71), part),
        "latents": draw_latents(jax.random.fold_in(jax.random.fold_in(keys[14], part), 71), part),
        "span_owner": draw_span_owner(jax.random.fold_in(jax.random.fold_in(keys[14], part), 71), part),
        "span_request": draw_span_request(jax.random.fold_in(jax.random.fold_in(keys[14], part), 71), part),
        "span_length": plant(jax.random.randint(part_keys[13], (SPANS,), 1, BLK + 1), jax.random.fold_in(part_keys[13], 1), 1, BLK).astype(jnp.int32),
    }


softmax_scale = 192.0 ** -0.5
gate_unit = 65536.0
row_block = 64


def half_expert(inputs, gate_up, down_proj):
    merged = jnp.dot(inputs, gate_up, preferred_element_type=jnp.float32)
    halfway = down_proj.shape[0]
    hidden = (jax.nn.silu(merged[:, :halfway]) * merged[:, halfway:]).astype(jnp.bfloat16)
    return jnp.dot(hidden, down_proj, preferred_element_type=jnp.float32).astype(jnp.bfloat16)


def whole_expert(inputs, w_gate_up, w_down, expert):
    first_half = half_expert(inputs, w_gate_up[2 * expert], w_down[2 * expert])
    other_half = half_expert(inputs, w_gate_up[2 * expert + 1], w_down[2 * expert + 1])
    return (first_half.astype(jnp.float32) + other_half.astype(jnp.float32)).astype(jnp.bfloat16)


def routed_layer(tokens, experts, gate_ints, w_gate_up, w_down):
    row_count = tokens.shape[0]
    padded = ((row_count + row_block - 1) // row_block) * row_block
    positions = jnp.arange(padded)

    def per_expert(expert):
        routed = jnp.any(experts == expert, axis=1)
        ordering = jnp.argsort(jnp.where(routed, 0, 1).astype(jnp.int32), stable=True).astype(jnp.int32)
        ordering = jnp.concatenate([ordering, jnp.zeros((padded - row_count,), jnp.int32)])
        active = routed[ordering] & (positions < row_count)

        def run_block(pieces):
            indices, alive_rows = pieces
            values = lax.cond(
                jnp.any(alive_rows),
                lambda unused: whole_expert(tokens[indices], w_gate_up, w_down, expert),
                lambda unused: jnp.zeros((row_block, tokens.shape[1]), jnp.bfloat16),
                0,
            )
            return jnp.where(alive_rows[:, None], values, jnp.zeros_like(values))

        values = lax.map(run_block, (ordering.reshape(-1, row_block), active.reshape(-1, row_block)))
        return jnp.zeros(tokens.shape, jnp.bfloat16).at[ordering].add(values.reshape(padded, -1))

    tables = lax.map(per_expert, jnp.arange(EXPERTS).astype(jnp.int32))
    picked = tables[experts, jnp.arange(row_count)[:, None]]
    weights = gate_ints.astype(jnp.float32) / gate_unit
    return jnp.einsum("rk,rkd->rd", weights, picked.astype(jnp.float32)).astype(jnp.bfloat16)


def reference(prefill_tokens, prefill_experts, prefill_gates, decode_rows, decode_experts, decode_gates, w_gate_up, w_down, queries, own_latent, latents, span_owner, span_request, span_length):
    prefill_out = routed_layer(prefill_tokens, prefill_experts, prefill_gates, w_gate_up, w_down)
    decode_out = routed_layer(decode_rows, decode_experts, decode_gates, w_gate_up, w_down)
    target = (span_owner * R_DEV + span_request).astype(jnp.int32)

    def per_span(pieces):
        latent, target_row, length = pieces
        query_rows = queries[target_row]
        expert_scores = jnp.dot(query_rows, latent.T, preferred_element_type=jnp.float32) * softmax_scale
        inside = jnp.arange(latent.shape[0]) < length
        highest = jnp.max(jnp.where(inside[None, :], expert_scores, -jnp.inf), axis=1)
        weights = jnp.where(inside[None, :], jnp.exp(expert_scores - highest[:, None]), 0.0)
        totals = jnp.sum(weights, axis=1)
        values = jnp.dot(weights.astype(jnp.bfloat16), latent[:, :KV], preferred_element_type=jnp.float32)
        return highest, totals, values

    span_max, span_total, span_value = lax.map(per_span, (latents, target, span_length))
    own_score = jnp.einsum("rhl,rl->rh", queries.astype(jnp.float32), own_latent.astype(jnp.float32)) * softmax_scale
    row_max = jnp.maximum(own_score, jax.ops.segment_max(span_max, target, num_segments=DEC_ROWS))
    factor = jnp.exp(span_max - row_max[target])
    own_factor = jnp.exp(own_score - row_max)
    totals = own_factor + jax.ops.segment_sum(factor * span_total, target, num_segments=DEC_ROWS)
    numerator = own_factor[:, :, None] * own_latent[:, None, :KV].astype(jnp.float32)
    numerator = numerator + jax.ops.segment_sum(factor[:, :, None] * span_value, target, num_segments=DEC_ROWS)
    context = (numerator / totals[:, :, None]).astype(jnp.bfloat16)
    return prefill_out, decode_out, context
```

```python
import functools

import jax
import jax.numpy as jnp
import numpy as np
from jax import lax
from jax.experimental import pallas as pl
from jax.experimental.pallas import tpu as pltpu
from jax.sharding import PartitionSpec as P

KV = 512
CAPC = 2

softmax_scale = 192.0 ** (-0.5)
gate_unit = 65536.0
AXIS = "expert"
VMEM_LIMIT = 56 * 1024 * 1024


def mlp_kernel(sizes, steps, *refs):
    count = len(sizes)
    x_refs = refs[:count]
    gate_ref, up_ref, down_ref = refs[count : count + 3]
    out_refs = refs[count + 3 : 2 * count + 3]
    rows_ref, total_ref = refs[2 * count + 3 :]
    step = pl.program_id(0)

    @pl.when(step == 0)
    def _():
        at = 0
        for x_ref, size in zip(x_refs, sizes):
            rows_ref[at : at + size, :] = x_ref[...]
            at += size

    rows = rows_ref[...]
    gate = jnp.dot(rows, gate_ref[...], preferred_element_type=jnp.float32)
    up = jnp.dot(rows, up_ref[...], preferred_element_type=jnp.float32)
    hidden = (jax.nn.silu(gate) * up).astype(jnp.bfloat16)
    width = down_ref.shape[1]
    tile = 1024 if width % 1024 == 0 else width

    for j in range(width // tile):
        cols = slice(j * tile, (j + 1) * tile)
        part = jnp.dot(hidden, down_ref[:, cols], preferred_element_type=jnp.float32)

        @pl.when(step == 0)
        def _(part=part, cols=cols):
            total_ref[:, cols] = part

        @pl.when((step > 0) & (step < steps - 1))
        def _(part=part, cols=cols):
            total_ref[:, cols] += part

        @pl.when(step == steps - 1)
        def _(part=part, cols=cols):
            value = (total_ref[:, cols] + part).astype(jnp.bfloat16)
            at = 0
            for out_ref, size in zip(out_refs, sizes):
                out_ref[:, cols] = value[at : at + size, :]
                at += size


def mlp(chunks, gate_up, down_proj):
    width = chunks[0].shape[1]
    half = down_proj.shape[0]
    tile = 256
    steps = half // tile
    sizes = tuple(c.shape[0] for c in chunks)
    rows = sum(sizes)
    x_specs = [pl.BlockSpec((size, width), lambda i: (0, 0)) for size in sizes]
    return pl.pallas_call(
        functools.partial(mlp_kernel, sizes, steps),
        grid=(steps,),
        in_specs=x_specs
        + [
            pl.BlockSpec((width, tile), lambda i: (0, i)),
            pl.BlockSpec((width, tile), lambda i: (0, i + steps)),
            pl.BlockSpec((tile, width), lambda i: (i, 0)),
        ],
        out_specs=[pl.BlockSpec((size, width), lambda i: (0, 0)) for size in sizes],
        out_shape=[jax.ShapeDtypeStruct((size, width), jnp.bfloat16) for size in sizes],
        scratch_shapes=[
            pltpu.VMEM((rows, width), jnp.bfloat16),
            pltpu.VMEM((rows, width), jnp.float32),
        ],
        compiler_params=pltpu.CompilerParams(vmem_limit_bytes=VMEM_LIMIT),
        cost_estimate=pl.CostEstimate(
            flops=6 * rows * width * half,
            bytes_accessed=6 * width * half + 4 * rows * width,
            transcendentals=rows * half,
        ),
        name="mlp",
    )(*chunks, gate_up, gate_up, down_proj)


def ship_kernel(source_ref, block_ref, out_ref):
    out_ref[...] = block_ref[...]


def ship_blocks(latents, source):
    slots = source.shape[0]
    shape = (1,) + latents.shape[1:]
    return pl.pallas_call(
        ship_kernel,
        grid_spec=pltpu.PrefetchScalarGridSpec(
            num_scalar_prefetch=1,
            grid=(slots,),
            in_specs=[pl.BlockSpec(shape, lambda i, source: (source[i], 0, 0))],
            out_specs=pl.BlockSpec(shape, lambda i, source: (i, 0, 0)),
        ),
        out_shape=jax.ShapeDtypeStruct((slots,) + latents.shape[1:], latents.dtype),
        name="ship",
    )(source, latents)


def attend_kernel(order_ref, start_ref, length_ref, query_ref, own_ref, latent_ref, out_ref):
    row = pl.program_id(0)
    query = query_ref[0]
    own = own_ref[0].astype(jnp.float32)
    own_score = (
        jnp.sum(query.astype(jnp.float32) * own, axis=1, keepdims=True) * softmax_scale
    )
    heads = query.shape[0]
    block = latent_ref.shape[1]

    def step(j, state):
        top, total, value = state
        slot = order_ref[j]
        latent = latent_ref[slot]
        scores = (
            lax.dot_general(
                query, latent, (((1,), (1,)), ((), ())), preferred_element_type=jnp.float32
            )
            * softmax_scale
        )
        inside = lax.broadcasted_iota(jnp.int32, (heads, block), 1) < length_ref[slot]
        span_max = jnp.max(jnp.where(inside, scores, -jnp.inf), axis=1, keepdims=True)
        weights = jnp.where(inside, jnp.exp(scores - span_max), 0.0)
        span_total = jnp.sum(weights, axis=1, keepdims=True)
        span_value = jnp.dot(
            weights.astype(jnp.bfloat16), latent[:, :KV], preferred_element_type=jnp.float32
        )
        higher = jnp.maximum(top, span_max)
        old = jnp.exp(top - higher)
        new = jnp.exp(span_max - higher)
        return (higher, old * total + new * span_total, old * value + new * span_value)

    state = (
        own_score,
        jnp.ones((heads, 1), jnp.float32),
        jnp.broadcast_to(own[:, :KV], (heads, KV)),
    )
    top, total, value = lax.fori_loop(start_ref[row], start_ref[row + 1], step, state)
    out_ref[0] = (value / total).astype(jnp.bfloat16)


def attend(order, start, lengths, queries, own_latent, latents):
    rows, heads, width = queries.shape
    slots, block, _ = latents.shape
    return pl.pallas_call(
        attend_kernel,
        grid_spec=pltpu.PrefetchScalarGridSpec(
            num_scalar_prefetch=3,
            grid=(rows,),
            in_specs=[
                pl.BlockSpec((1, heads, width), lambda i, *_: (i, 0, 0)),
                pl.BlockSpec((1, 1, width), lambda i, *_: (i, 0, 0)),
                pl.BlockSpec((slots, block, width), lambda i, *_: (0, 0, 0)),
            ],
            out_specs=pl.BlockSpec((1, heads, KV), lambda i, *_: (i, 0, 0)),
        ),
        out_shape=jax.ShapeDtypeStruct((rows, heads, KV), jnp.bfloat16),
        compiler_params=pltpu.CompilerParams(vmem_limit_bytes=VMEM_LIMIT),
        cost_estimate=pl.CostEstimate(
            flops=4 * slots * heads * block * width,
            bytes_accessed=2 * (rows * heads * (width + KV) + slots * block * width),
            transcendentals=slots * heads * block,
        ),
        name="attend",
    )(order, start, lengths, queries, own_latent.reshape(rows, 1, width), latents)


def dense_gates(experts, gates, expert_count):
    named = experts[:, :, None] == jnp.arange(expert_count)[None, None, :]
    return jnp.sum(jnp.where(named, gates[:, :, None], 0), axis=1)


def per_device(
    prefill_tokens,
    prefill_experts,
    prefill_gates,
    decode_rows,
    decode_experts,
    decode_gates,
    w_gate_up,
    w_down,
    queries,
    own_latent,
    latents,
    span_owner,
    span_request,
    span_length,
):
    devices = lax.axis_size(AXIS)
    chips = devices // 2
    half = chips // 2
    gate_up = w_gate_up[0]
    down_proj = w_down[0]
    prefill_count = prefill_tokens.shape[0]
    decode_count = decode_rows.shape[0]
    row_count = prefill_count + decode_count
    split = prefill_count

    ring = list(range(0, chips, 2)) + list(range(1, chips, 2))[::-1]
    place_of = np.zeros(chips, np.int32)
    for i, chip in enumerate(ring):
        place_of[chip] = i
    ahead = [
        (2 * ring[i] + c, 2 * ring[(i + 1) % chips] + c) for i in range(chips) for c in range(2)
    ]
    back = [(b, a) for a, b in ahead]
    across = [(i, i ^ 1) for i in range(devices)]
    me = lax.axis_index(AXIS)
    my_chip = me // 2
    my_core = me % 2
    place = jnp.asarray(place_of)[my_chip]

    def device_at(shift):
        return 2 * jnp.asarray(np.array(ring, np.int32))[(place + shift + chips) % chips] + my_core

    gates = jnp.concatenate(
        [
            dense_gates(prefill_experts, prefill_gates, chips),
            dense_gates(decode_experts, decode_gates, chips),
        ],
        axis=0,
    )
    span_count = span_owner.shape[0]
    block_rows = latents.shape[1]
    codes = (span_owner * decode_count + span_request) * (block_rows + 1) + span_length
    small = jnp.concatenate([gates.T.reshape(-1), codes]).astype(jnp.int32)
    small = lax.all_gather(small, AXIS, tiled=False)
    gate_table = small[:, : chips * row_count].reshape(devices, chips, row_count)
    gate_table = (
        lax.dynamic_index_in_dim(gate_table, my_chip, 1, keepdims=False).astype(jnp.float32)
        / gate_unit
    )
    all_codes = small[:, chips * row_count :]

    numbered = jnp.arange(span_count)
    earlier = (span_owner[None, :] == span_owner[:, None]) & (numbered[None, :] < numbered[:, None])
    span_rank = jnp.sum(earlier, axis=1)
    slot_of = span_owner * CAPC + span_rank
    slots = devices * CAPC
    source = jnp.sum(
        jnp.where(slot_of[None, :] == jnp.arange(slots)[:, None], numbered[None, :], 0), axis=1
    ).astype(jnp.int32)
    shipped = ship_blocks(latents, source)

    own_rows = jnp.concatenate([prefill_tokens, decode_rows], axis=0)
    front = [own_rows]
    rear = [own_rows]
    for s in range(1, half):
        front.append(lax.ppermute(front[-1], AXIS, ahead))
        rear.append(lax.ppermute(rear[-1], AXIS, back))
    front.append(lax.ppermute(front[-1][:split], AXIS, ahead))
    rear.append(lax.ppermute(rear[-1][split:], AXIS, back))

    block_latents = lax.optimization_barrier((shipped, front[half - 1], rear[half - 1]))[0]
    block_latents = lax.all_to_all(block_latents, AXIS, split_axis=0, concat_axis=0, tiled=True)

    own_part = {}
    for s in range(half + 1):
        mine = [own_rows] if s == 0 else [front[s], rear[s]]
        other = [lax.ppermute(c, AXIS, across) for c in mine]
        parts = mlp(mine + other, gate_up, down_proj)
        count = len(mine)
        for k in range(count):
            own_part[(s, k)] = (parts[k], lax.ppermute(parts[count + k], AXIS, across))

    def contribution(s, k, lo, hi):
        part, from_other = own_part[(s, k)]
        both = (part.astype(jnp.float32) + from_other.astype(jnp.float32)).astype(jnp.bfloat16)
        shift = (-s, s)[k] if s else 0
        weight = lax.dynamic_index_in_dim(gate_table, device_at(shift), 0, keepdims=False)
        return weight[lo:hi, None] * both.astype(jnp.float32)

    up = contribution(half, 0, 0, split).astype(jnp.bfloat16)
    down = contribution(half, 1, split, row_count).astype(jnp.bfloat16)
    for s in range(half - 1, 0, -1):
        up = lax.ppermute(up, AXIS, ahead).astype(jnp.float32)
        down = lax.ppermute(down, AXIS, back).astype(jnp.float32)
        up_own = contribution(s, 1, 0, row_count)
        down_own = contribution(s, 0, 0, row_count)
        if s == half - 1:
            up = jnp.pad(up, ((0, row_count - split), (0, 0)))
            down = jnp.pad(down, ((split, 0), (0, 0)))
        up = (up + up_own).astype(jnp.bfloat16)
        down = (down + down_own).astype(jnp.bfloat16)
    up = lax.ppermute(up, AXIS, ahead).astype(jnp.float32)
    down = lax.ppermute(down, AXIS, back).astype(jnp.float32)
    out = (contribution(0, 0, 0, row_count) + up + down).astype(jnp.bfloat16)
    prefill_out = out[:split]
    decode_out = out[split:]

    lengths = all_codes % (block_rows + 1)
    targets = all_codes // (block_rows + 1)
    owners = targets // decode_count
    requests = targets % decode_count
    here = owners == me
    rank = jnp.cumsum(here.astype(jnp.int32), axis=1) - 1
    taken = here[:, None, :] & (rank[:, None, :] == jnp.arange(CAPC)[None, :, None])
    slot_length = jnp.sum(jnp.where(taken, lengths[:, None, :], 0), axis=2).reshape(-1)
    slot_request = jnp.sum(jnp.where(taken, requests[:, None, :], 0), axis=2).reshape(-1)
    key = jnp.where(slot_length > 0, slot_request, decode_count)
    index = jnp.arange(slots)
    before = (key[None, :] < key[:, None]) | (
        (key[None, :] == key[:, None]) & (index[None, :] < index[:, None])
    )
    position = jnp.sum(before, axis=1)
    order = jnp.sum(
        jnp.where(position[None, :] == index[:, None], index[None, :], 0), axis=1
    ).astype(jnp.int32)
    start = jnp.sum(key[None, :] < jnp.arange(decode_count + 1)[:, None], axis=1).astype(jnp.int32)
    context = attend(
        order, start, slot_length.astype(jnp.int32), queries, own_latent, block_latents
    )
    return (prefill_out, decode_out, context)


def solution(mesh):
    rows = P(("groups", "expert"), None)
    blocks = P(("groups", "expert"), None, None)
    line = P(("groups", "expert"))
    weights = P("expert", None, None)
    return jax.shard_map(
        per_device,
        mesh=mesh,
        in_specs=(rows,) * 6 + (weights, weights, blocks, rows, blocks, line, line, line),
        out_specs=(rows, rows, blocks),
        check_vma=False,
    )
```

```python
import functools

import jax
import jax.numpy as jnp
import numpy as np
from jax import lax
from jax.experimental import pallas as pl
from jax.experimental.pallas import tpu as pltpu
from jax.sharding import PartitionSpec as P

KV = 512
CAPC = 2

softmax_scale = 192.0 ** (-0.5)
gate_unit = 65536.0
AXIS = "expert"
WAIT_STEP = 1
VMEM_LIMIT = 16 << 20


def mlp_kernel(sizes, tile, *refs):
    count = len(sizes)
    x_refs = refs[:count]
    up_hbm, down_hbm, mine_hbm, other_hbm = refs[count : count + 4]
    rows_ref, up_ref, down_ref, part_ref, x_sems, up_sems, down_sems, out_sems = refs[count + 4 :]
    width = up_hbm.shape[0]
    half = down_hbm.shape[0]
    tiles = width // tile
    size = mine_hbm.shape[0]
    spans = [pl.ds(k * tile, tile) for k in range(tiles)]
    starts = [sum(sizes[:c]) for c in range(count)]
    x_copies = [
        [
            pltpu.make_async_copy(
                x_refs[c].at[:, spans[k]],
                rows_ref.at[pl.ds(starts[c], sizes[c]), spans[k]],
                x_sems.at[c, k],
            )
            for c in range(count)
        ]
        for k in range(tiles)
    ]
    up_copies = [
        pltpu.make_async_copy(up_hbm.at[s], up_ref.at[s], up_sems.at[k])
        for k, s in enumerate(spans)
    ]
    down_copies = [
        pltpu.make_async_copy(down_hbm.at[:, s], down_ref.at[:, s], down_sems.at[k])
        for k, s in enumerate(spans)
    ]
    for k in range(tiles):
        for copy in x_copies[k]:
            copy.start()
        up_copies[k].start()
    for copy in down_copies:
        copy.start()
    merged = None
    for k in range(tiles):
        for copy in x_copies[k]:
            copy.wait()
        up_copies[k].wait()
        cols = slice(k * tile, (k + 1) * tile)
        part = jnp.dot(rows_ref[:, cols], up_ref[cols, :], preferred_element_type=jnp.float32)
        merged = part if merged is None else merged + part
    hidden = (jax.nn.silu(merged[:, :half]) * merged[:, half:]).astype(jnp.bfloat16)
    out_copies = []
    for n, s in enumerate(spans):
        down_copies[n].wait()
        cols = slice(n * tile, (n + 1) * tile)
        part = jnp.dot(hidden, down_ref[:, cols], preferred_element_type=jnp.float32)
        part_ref[:, cols] = part.astype(jnp.bfloat16)
        for c, target in enumerate((mine_hbm, other_hbm)):
            copy = pltpu.make_async_copy(
                part_ref.at[pl.ds(c * size, size), s], target.at[:, s], out_sems.at[c, n]
            )
            copy.start()
            out_copies.append(copy)
    for copy in out_copies:
        copy.wait()


def mlp(mine, other, gate_up, down_proj, tile=1024):
    chunks = mine + other
    width, both = gate_up.shape
    half = down_proj.shape[0]
    tile = tile if width % tile == 0 else width
    tiles = width // tile
    sizes = tuple(c.shape[0] for c in chunks)
    rows = sum(sizes)
    anywhere = pl.BlockSpec(memory_space=pltpu.HBM)
    dma = pltpu.SemaphoreType.DMA
    return pl.pallas_call(
        functools.partial(mlp_kernel, sizes, tile),
        in_specs=[anywhere] * (len(chunks) + 2),
        out_specs=[anywhere, anywhere],
        out_shape=[jax.ShapeDtypeStruct((rows // 2, width), jnp.bfloat16)] * 2,
        scratch_shapes=[
            pltpu.VMEM((rows, width), jnp.bfloat16),
            pltpu.VMEM((width, both), jnp.bfloat16),
            pltpu.VMEM((half, width), jnp.bfloat16),
            pltpu.VMEM((rows, width), jnp.bfloat16),
            dma((len(chunks), tiles)),
            dma((tiles,)),
            dma((tiles,)),
            dma((2, tiles)),
        ],
        compiler_params=pltpu.CompilerParams(vmem_limit_bytes=44 << 20),
        cost_estimate=pl.CostEstimate(
            flops=6 * rows * width * half,
            bytes_accessed=6 * width * half + 4 * rows * width,
            transcendentals=rows * half,
        ),
        name="mlp",
    )(*chunks, gate_up, down_proj)


def ship_kernel(source_ref, block_ref, out_ref):
    for i in range(out_ref.shape[0]):
        out_ref[i] = block_ref[source_ref[i]]


def ship_blocks(latents, source):
    slots = source.shape[0]
    resident = pl.BlockSpec(memory_space=pltpu.VMEM)
    return pl.pallas_call(
        ship_kernel,
        in_specs=[pl.BlockSpec(memory_space=pltpu.SMEM), resident],
        out_specs=resident,
        out_shape=jax.ShapeDtypeStruct((slots,) + latents.shape[1:], latents.dtype),
        compiler_params=pltpu.CompilerParams(vmem_limit_bytes=16 << 20),
        cost_estimate=pl.CostEstimate(
            flops=0, bytes_accessed=6 * latents.size, transcendentals=0
        ),
        name="ship",
    )(source, latents)


def attend_kernel(order_ref, start_ref, length_ref, query_ref, own_ref, latent_ref, out_ref):
    row = pl.program_id(0)
    query = query_ref[0]
    own = own_ref[0].astype(jnp.float32)
    own_score = (
        jnp.sum(query.astype(jnp.float32) * own, axis=1, keepdims=True) * softmax_scale
    )
    heads = query.shape[0]
    block = latent_ref.shape[1]

    def step(j, state):
        top, total, value = state
        slot = order_ref[j]
        latent = latent_ref[slot]
        scores = (
            lax.dot_general(
                query, latent, (((1,), (1,)), ((), ())), preferred_element_type=jnp.float32
            )
            * softmax_scale
        )
        inside = lax.broadcasted_iota(jnp.int32, (heads, block), 1) < length_ref[slot]
        span_max = jnp.max(jnp.where(inside, scores, -jnp.inf), axis=1, keepdims=True)
        weights = jnp.where(inside, jnp.exp(scores - span_max), 0.0)
        span_total = jnp.sum(weights, axis=1, keepdims=True)
        span_value = jnp.dot(
            weights.astype(jnp.bfloat16), latent[:, :KV], preferred_element_type=jnp.float32
        )
        higher = jnp.maximum(top, span_max)
        old = jnp.exp(top - higher)
        new = jnp.exp(span_max - higher)
        return (higher, old * total + new * span_total, old * value + new * span_value)

    state = (
        own_score,
        jnp.ones((heads, 1), jnp.float32),
        jnp.broadcast_to(own[:, :KV], (heads, KV)),
    )
    top, total, value = lax.fori_loop(start_ref[row], start_ref[row + 1], step, state)
    out_ref[0] = (value / total).astype(jnp.bfloat16)


def attend(order, start, lengths, queries, own_latent, latents, first, rows):
    _, heads, width = queries.shape
    slots, block, _ = latents.shape
    own_latent = own_latent.reshape(own_latent.shape[0], 1, width)
    return pl.pallas_call(
        attend_kernel,
        grid_spec=pltpu.PrefetchScalarGridSpec(
            num_scalar_prefetch=3,
            grid=(rows,),
            in_specs=[
                pl.BlockSpec((1, heads, width), lambda i, *_: (i + first, 0, 0)),
                pl.BlockSpec((1, 1, width), lambda i, *_: (i + first, 0, 0)),
                pl.BlockSpec((slots, block, width), lambda i, *_: (0, 0, 0)),
            ],
            out_specs=pl.BlockSpec((1, heads, KV), lambda i, *_: (i, 0, 0)),
        ),
        out_shape=jax.ShapeDtypeStruct((rows, heads, KV), jnp.bfloat16),
        compiler_params=pltpu.CompilerParams(vmem_limit_bytes=VMEM_LIMIT),
        cost_estimate=pl.CostEstimate(
            flops=2 * slots * heads * block * width,
            bytes_accessed=2 * (rows * heads * (width + KV) + slots * block * width),
            transcendentals=slots * heads * block,
        ),
        name="attend",
    )(order, start[first : first + rows + 1], lengths, queries, own_latent, latents)


def dense_gates(experts, gates, expert_count):
    named = experts[:, :, None] == jnp.arange(expert_count)[None, None, :]
    return jnp.sum(jnp.where(named, gates[:, :, None], 0), axis=1)


def per_device(
    prefill_tokens,
    prefill_experts,
    prefill_gates,
    decode_rows,
    decode_experts,
    decode_gates,
    w_gate_up,
    w_down,
    queries,
    own_latent,
    latents,
    span_owner,
    span_request,
    span_length,
):
    devices = lax.axis_size(AXIS)
    chips = devices // 2
    half = chips // 2
    gate_up = w_gate_up[0]
    down_proj = w_down[0]
    prefill_count = prefill_tokens.shape[0]
    decode_count = decode_rows.shape[0]
    row_count = prefill_count + decode_count
    split = prefill_count

    ring = list(range(0, chips, 2)) + list(range(1, chips, 2))[::-1]
    place_of = np.zeros(chips, np.int32)
    for i, chip in enumerate(ring):
        place_of[chip] = i
    ahead = [
        (2 * ring[i] + c, 2 * ring[(i + 1) % chips] + c) for i in range(chips) for c in range(2)
    ]
    back = [(b, a) for a, b in ahead]
    across = [(i, i ^ 1) for i in range(devices)]
    me = lax.axis_index(AXIS)
    my_chip = me // 2
    my_core = me % 2
    place = jnp.asarray(place_of)[my_chip]

    def device_at(shift):
        return 2 * jnp.asarray(np.array(ring, np.int32))[(place + shift + chips) % chips] + my_core

    span_count = span_owner.shape[0]
    block_rows = latents.shape[1]
    slots = devices * CAPC
    numbered = jnp.arange(span_count)
    earlier = (span_owner[None, :] == span_owner[:, None]) & (numbered[None, :] < numbered[:, None])
    span_rank = jnp.sum(earlier, axis=1)
    slot_of = span_owner * CAPC + span_rank
    placed = slot_of[None, :] == jnp.arange(slots)[:, None]
    source = jnp.sum(jnp.where(placed, numbered[None, :], 0), axis=1).astype(jnp.int32)
    codes = span_request * (block_rows + 1) + span_length
    slot_codes = jnp.sum(jnp.where(placed, codes[None, :], 0), axis=1).astype(jnp.int32)

    gates = jnp.concatenate(
        [
            dense_gates(prefill_experts, prefill_gates, chips),
            dense_gates(decode_experts, decode_gates, chips),
        ],
        axis=0,
    )
    small = jnp.concatenate(
        [jnp.repeat(gates.T, 2, axis=0), slot_codes.reshape(devices, CAPC)], axis=1
    ).astype(jnp.int32)
    small = lax.all_to_all(small, AXIS, split_axis=0, concat_axis=0, tiled=True)
    gate_table = small[:, :row_count].astype(jnp.float32) / gate_unit
    slot_codes = small[:, row_count:].reshape(-1)
    slot_length = slot_codes % (block_rows + 1)
    slot_request = slot_codes // (block_rows + 1)

    shipped = ship_blocks(latents, source)

    own_rows = jnp.concatenate([prefill_tokens, decode_rows], axis=0)
    own_other = lax.ppermute(own_rows, AXIS, across)
    a = lax.ppermute(own_rows, AXIS, ahead)
    b = lax.ppermute(own_rows, AXIS, back)
    a, b, shipped, gate_table = lax.optimization_barrier((a, b, shipped, gate_table))
    arrived = [(a, b)]
    parts = {}
    for s in range(1, half + 1):
        a, b = arrived[-1]
        if s < half:
            if s == half - 1:
                next_a = lax.ppermute(a[:split], AXIS, ahead)
                next_b = lax.ppermute(b[split:], AXIS, back)
                block_latents = lax.all_to_all(
                    shipped, AXIS, split_axis=0, concat_axis=0, tiled=True
                )
            else:
                next_a = lax.ppermute(a, AXIS, ahead)
                next_b = lax.ppermute(b, AXIS, back)
        mine = [a, b]
        other = [lax.ppermute(c, AXIS, across) for c in mine]
        if s == 1:
            mine = mine + [own_rows]
            other = other + [own_other]
        part, for_other = mlp(mine, other, gate_up, down_proj)
        if s < half:
            next_a, next_b, part, for_other, shipped = lax.optimization_barrier(
                (next_a, next_b, part, for_other, shipped)
            )
            arrived.append((next_a, next_b))
        parts[s] = (part, lax.ppermute(for_other, AXIS, across))

    def contribution(s, k):
        part, from_other = parts[max(s, 1)]
        size = split if s == half else row_count
        lo = 2 * size if s == 0 else k * size
        both = part[lo : lo + size].astype(jnp.float32) + from_other[lo : lo + size].astype(
            jnp.float32
        )
        both = both.astype(jnp.bfloat16).astype(jnp.float32)
        shift = (-s, s)[k] if s else 0
        weight = lax.dynamic_index_in_dim(gate_table, device_at(shift), 0, keepdims=False)
        if s == half:
            weight = (weight[:split], weight[split:])[k]
        return weight[:, None] * both

    key = jnp.where(slot_length > 0, slot_request, decode_count)
    index = jnp.arange(slots)
    before = (key[None, :] < key[:, None]) | (
        (key[None, :] == key[:, None]) & (index[None, :] < index[:, None])
    )
    position = jnp.sum(before, axis=1)
    order = jnp.sum(
        jnp.where(position[None, :] == index[:, None], index[None, :], 0), axis=1
    ).astype(jnp.int32)
    start = jnp.sum(key[None, :] < jnp.arange(decode_count + 1)[:, None], axis=1).astype(jnp.int32)
    first_rows = decode_count // 2

    up = contribution(half, 0).astype(jnp.bfloat16)
    down = contribution(half, 1).astype(jnp.bfloat16)
    for s in range(half - 1, -1, -1):
        up, down = lax.optimization_barrier((up, down))
        up = lax.ppermute(up, AXIS, ahead)
        down = lax.ppermute(down, AXIS, back)
        up, down = lax.optimization_barrier((up, down))
        if s == half - WAIT_STEP:
            up, down, block_latents = lax.optimization_barrier((up, down, block_latents))
        up = up.astype(jnp.float32)
        down = down.astype(jnp.float32)
        if s == half - 1:
            up = jnp.pad(up, ((0, row_count - split), (0, 0)))
            down = jnp.pad(down, ((split, 0), (0, 0)))
        if s:
            up = (up + contribution(s, 1)).astype(jnp.bfloat16)
            down = (down + contribution(s, 0)).astype(jnp.bfloat16)
        if s == 1:
            early = attend(
                order, start, slot_length, queries, own_latent, block_latents, 0, first_rows
            )
            up, down, early = lax.optimization_barrier((up, down, early))
            late = attend(
                order,
                start,
                slot_length,
                queries,
                own_latent,
                block_latents,
                first_rows,
                decode_count - first_rows,
            )
            context = jnp.concatenate([early, late], axis=0)
    out = (contribution(0, 0) + up + down).astype(jnp.bfloat16)
    prefill_out = out[:split]
    decode_out = out[split:]
    return (prefill_out, decode_out, context)


def solution(mesh):
    rows = P(("groups", "expert"), None)
    blocks = P(("groups", "expert"), None, None)
    line = P(("groups", "expert"))
    weights = P("expert", None, None)
    return jax.shard_map(
        per_device,
        mesh=mesh,
        in_specs=(rows,) * 6 + (weights, weights, blocks, rows, blocks, line, line, line),
        out_specs=(rows, rows, blocks),
        check_vma=False,
    )
```

```python
import functools

import jax
import jax.numpy as jnp
import numpy as np
from jax import lax
from jax.experimental import pallas as pl
from jax.experimental.pallas import tpu as pltpu
from jax.sharding import PartitionSpec as P

KV = 512
CAPC = 2

softmax_scale = 192.0 ** (-0.5)
gate_unit = 65536.0
AXIS = "expert"
VMEM_LIMIT = 16 << 20


def mlp_kernel(sizes, tile, *refs):
    count = len(sizes)
    x_refs = refs[:count]
    up_hbm, down_hbm, mine_hbm, other_hbm = refs[count : count + 4]
    rows_ref, up_ref, down_ref, part_ref, x_sems, up_sems, down_sems, out_sems = refs[count + 4 :]
    width = up_hbm.shape[0]
    half = down_hbm.shape[0]
    tiles = width // tile
    size = mine_hbm.shape[0]
    spans = [pl.ds(k * tile, tile) for k in range(tiles)]
    starts = [sum(sizes[:c]) for c in range(count)]
    x_copies = [
        [
            pltpu.make_async_copy(
                x_refs[c].at[:, spans[k]],
                rows_ref.at[pl.ds(starts[c], sizes[c]), spans[k]],
                x_sems.at[c, k],
            )
            for c in range(count)
        ]
        for k in range(tiles)
    ]
    up_copies = [
        pltpu.make_async_copy(up_hbm.at[s], up_ref.at[s], up_sems.at[k])
        for k, s in enumerate(spans)
    ]
    down_copies = [
        pltpu.make_async_copy(down_hbm.at[:, s], down_ref.at[:, s], down_sems.at[k])
        for k, s in enumerate(spans)
    ]
    for k in range(tiles):
        for copy in x_copies[k]:
            copy.start()
        up_copies[k].start()
    for copy in down_copies:
        copy.start()
    merged = None
    for k in range(tiles):
        for copy in x_copies[k]:
            copy.wait()
        up_copies[k].wait()
        cols = slice(k * tile, (k + 1) * tile)
        part = jnp.dot(rows_ref[:, cols], up_ref[cols, :], preferred_element_type=jnp.float32)
        merged = part if merged is None else merged + part
    hidden = (jax.nn.silu(merged[:, :half]) * merged[:, half:]).astype(jnp.bfloat16)
    out_copies = []
    for n, s in enumerate(spans):
        down_copies[n].wait()
        cols = slice(n * tile, (n + 1) * tile)
        part = jnp.dot(hidden, down_ref[:, cols], preferred_element_type=jnp.float32)
        part_ref[:, cols] = part.astype(jnp.bfloat16)
        for c, target in enumerate((mine_hbm, other_hbm)):
            copy = pltpu.make_async_copy(
                part_ref.at[pl.ds(c * size, size), s], target.at[:, s], out_sems.at[c, n]
            )
            copy.start()
            out_copies.append(copy)
    for copy in out_copies:
        copy.wait()


def mlp(mine, other, gate_up, down_proj, tile=1024):
    chunks = mine + other
    width, both = gate_up.shape
    half = down_proj.shape[0]
    tile = tile if width % tile == 0 else width
    tiles = width // tile
    sizes = tuple(c.shape[0] for c in chunks)
    rows = sum(sizes)
    anywhere = pl.BlockSpec(memory_space=pltpu.HBM)
    dma = pltpu.SemaphoreType.DMA
    return pl.pallas_call(
        functools.partial(mlp_kernel, sizes, tile),
        in_specs=[anywhere] * (len(chunks) + 2),
        out_specs=[anywhere, anywhere],
        out_shape=[jax.ShapeDtypeStruct((rows // 2, width), jnp.bfloat16)] * 2,
        scratch_shapes=[
            pltpu.VMEM((rows, width), jnp.bfloat16),
            pltpu.VMEM((width, both), jnp.bfloat16),
            pltpu.VMEM((half, width), jnp.bfloat16),
            pltpu.VMEM((rows, width), jnp.bfloat16),
            dma((len(chunks), tiles)),
            dma((tiles,)),
            dma((tiles,)),
            dma((2, tiles)),
        ],
        compiler_params=pltpu.CompilerParams(vmem_limit_bytes=44 << 20),
        cost_estimate=pl.CostEstimate(
            flops=6 * rows * width * half,
            bytes_accessed=6 * width * half + 4 * rows * width,
            transcendentals=rows * half,
        ),
        name="mlp",
    )(*chunks, gate_up, down_proj)


def ship_kernel(source_ref, block_ref, out_ref):
    for i in range(out_ref.shape[0]):
        out_ref[i] = block_ref[source_ref[i]]


def ship_blocks(latents, source):
    slots = source.shape[0]
    resident = pl.BlockSpec(memory_space=pltpu.VMEM)
    return pl.pallas_call(
        ship_kernel,
        in_specs=[pl.BlockSpec(memory_space=pltpu.SMEM), resident],
        out_specs=resident,
        out_shape=jax.ShapeDtypeStruct((slots,) + latents.shape[1:], latents.dtype),
        compiler_params=pltpu.CompilerParams(vmem_limit_bytes=16 << 20),
        cost_estimate=pl.CostEstimate(
            flops=0, bytes_accessed=6 * latents.size, transcendentals=0
        ),
        name="ship",
    )(source, latents)


def attend_kernel(order_ref, start_ref, length_ref, query_ref, own_ref, latent_ref, out_ref):
    row = pl.program_id(0)
    query = query_ref[0]
    own = own_ref[0].astype(jnp.float32)
    own_score = (
        jnp.sum(query.astype(jnp.float32) * own, axis=1, keepdims=True) * softmax_scale
    )
    heads = query.shape[0]
    block = latent_ref.shape[1]

    def step(j, state):
        top, total, value = state
        slot = order_ref[j]
        latent = latent_ref[slot]
        scores = (
            lax.dot_general(
                query, latent, (((1,), (1,)), ((), ())), preferred_element_type=jnp.float32
            )
            * softmax_scale
        )
        inside = lax.broadcasted_iota(jnp.int32, (heads, block), 1) < length_ref[slot]
        span_max = jnp.max(jnp.where(inside, scores, -jnp.inf), axis=1, keepdims=True)
        weights = jnp.where(inside, jnp.exp(scores - span_max), 0.0)
        span_total = jnp.sum(weights, axis=1, keepdims=True)
        span_value = jnp.dot(
            weights.astype(jnp.bfloat16), latent[:, :KV], preferred_element_type=jnp.float32
        )
        higher = jnp.maximum(top, span_max)
        old = jnp.exp(top - higher)
        new = jnp.exp(span_max - higher)
        return (higher, old * total + new * span_total, old * value + new * span_value)

    state = (
        own_score,
        jnp.ones((heads, 1), jnp.float32),
        jnp.broadcast_to(own[:, :KV], (heads, KV)),
    )
    top, total, value = lax.fori_loop(start_ref[row], start_ref[row + 1], step, state)
    out_ref[0] = (value / total).astype(jnp.bfloat16)


def attend(order, start, lengths, queries, own_latent, latents, first, rows):
    _, heads, width = queries.shape
    slots, block, _ = latents.shape
    own_latent = own_latent.reshape(own_latent.shape[0], 1, width)
    return pl.pallas_call(
        attend_kernel,
        grid_spec=pltpu.PrefetchScalarGridSpec(
            num_scalar_prefetch=3,
            grid=(rows,),
            in_specs=[
                pl.BlockSpec((1, heads, width), lambda i, *_: (i + first, 0, 0)),
                pl.BlockSpec((1, 1, width), lambda i, *_: (i + first, 0, 0)),
                pl.BlockSpec((slots, block, width), lambda i, *_: (0, 0, 0)),
            ],
            out_specs=pl.BlockSpec((1, heads, KV), lambda i, *_: (i, 0, 0)),
        ),
        out_shape=jax.ShapeDtypeStruct((rows, heads, KV), jnp.bfloat16),
        compiler_params=pltpu.CompilerParams(vmem_limit_bytes=VMEM_LIMIT),
        cost_estimate=pl.CostEstimate(
            flops=2 * slots * heads * block * width,
            bytes_accessed=2 * (rows * heads * (width + KV) + slots * block * width),
            transcendentals=slots * heads * block,
        ),
        name="attend",
    )(order, start[first : first + rows + 1], lengths, queries, own_latent, latents)


def dense_gates(experts, gates, expert_count):
    named = experts[:, :, None] == jnp.arange(expert_count)[None, None, :]
    return jnp.sum(jnp.where(named, gates[:, :, None], 0), axis=1)


def per_device(
    prefill_tokens,
    prefill_experts,
    prefill_gates,
    decode_rows,
    decode_experts,
    decode_gates,
    w_gate_up,
    w_down,
    queries,
    own_latent,
    latents,
    span_owner,
    span_request,
    span_length,
):
    devices = lax.axis_size(AXIS)
    chips = devices // 2
    half = chips // 2
    gate_up = w_gate_up[0]
    down_proj = w_down[0]
    prefill_count = prefill_tokens.shape[0]
    decode_count = decode_rows.shape[0]
    row_count = prefill_count + decode_count
    split = prefill_count

    ring = list(range(0, chips, 2)) + list(range(1, chips, 2))[::-1]
    place_of = np.zeros(chips, np.int32)
    for i, chip in enumerate(ring):
        place_of[chip] = i
    ahead = [
        (2 * ring[i] + c, 2 * ring[(i + 1) % chips] + c) for i in range(chips) for c in range(2)
    ]
    back = [(b, a) for a, b in ahead]
    across = [(i, i ^ 1) for i in range(devices)]
    me = lax.axis_index(AXIS)
    neighbours = np.zeros((devices, chips), np.int32)
    for device in range(devices):
        for shift in range(chips):
            chip = ring[(place_of[device // 2] + shift) % chips]
            neighbours[device, shift] = 2 * chip + device % 2

    span_count = span_owner.shape[0]
    block_rows = latents.shape[1]
    slots = devices * CAPC
    numbered = jnp.arange(span_count)
    earlier = (span_owner[None, :] == span_owner[:, None]) & (numbered[None, :] < numbered[:, None])
    span_rank = jnp.sum(earlier, axis=1)
    slot_of = span_owner * CAPC + span_rank
    placed = slot_of[None, :] == jnp.arange(slots)[:, None]
    source = jnp.sum(jnp.where(placed, numbered[None, :], 0), axis=1).astype(jnp.int32)
    codes = span_request * (block_rows + 1) + span_length
    slot_codes = jnp.sum(jnp.where(placed, codes[None, :], 0), axis=1).astype(jnp.int32)

    gates = jnp.concatenate(
        [
            dense_gates(prefill_experts, prefill_gates, chips),
            dense_gates(decode_experts, decode_gates, chips),
        ],
        axis=0,
    )
    small = jnp.concatenate(
        [jnp.repeat(gates.T, 2, axis=0), slot_codes.reshape(devices, CAPC)], axis=1
    ).astype(jnp.int32)
    small = lax.all_to_all(small, AXIS, split_axis=0, concat_axis=0, tiled=True)
    at_shift = lax.dynamic_index_in_dim(jnp.asarray(neighbours), me, 0, keepdims=False)
    picked = at_shift[:, None] == jnp.arange(devices)[None, :]
    shift_gates = jnp.sum(jnp.where(picked[:, :, None], small[None, :, :row_count], 0), axis=1)
    shift_gates = shift_gates.astype(jnp.float32) / gate_unit
    slot_codes = small[:, row_count:].reshape(-1)
    slot_length = slot_codes % (block_rows + 1)
    slot_request = slot_codes // (block_rows + 1)

    shipped = ship_blocks(latents, source)

    own = [prefill_tokens, decode_rows]
    own_other = [lax.ppermute(c, AXIS, across) for c in own]
    front = [lax.ppermute(c, AXIS, ahead) for c in own]
    rear = [lax.ppermute(c, AXIS, back) for c in own]
    front, rear, shipped = lax.optimization_barrier((front, rear, shipped))
    parts = {}
    for s in range(1, half + 1):
        if s == half - 1:
            next_front = [lax.ppermute(front[0], AXIS, ahead)]
            next_rear = [lax.ppermute(rear[1], AXIS, back)]
        elif s < half:
            next_front = [lax.ppermute(c, AXIS, ahead) for c in front]
            next_rear = [lax.ppermute(c, AXIS, back) for c in rear]
        mine = front + rear
        other = [lax.ppermute(c, AXIS, across) for c in mine]
        if s == 1:
            mine = mine + own
            other = other + own_other
        part, for_other = mlp(mine, other, gate_up, down_proj)
        if s < half:
            front, rear, part, for_other, shipped, shift_gates = lax.optimization_barrier(
                (next_front, next_rear, part, for_other, shipped, shift_gates)
            )
        parts[s] = (part, lax.ppermute(for_other, AXIS, across))
    block_latents = lax.all_to_all(shipped, AXIS, split_axis=0, concat_axis=0, tiled=True)

    def contribution(s, k):
        part, from_other = parts[max(s, 1)]
        size = split if s == half else row_count
        lo = 2 * row_count if s == 0 else k * size
        both = part[lo : lo + size].astype(jnp.float32) + from_other[lo : lo + size].astype(
            jnp.float32
        )
        weight = shift_gates[((-s, s)[k] + chips) % chips]
        if s == half:
            weight = (weight[:split], weight[split:])[k]
        return (weight[:, None] * both).astype(jnp.bfloat16)

    key = jnp.where(slot_length > 0, slot_request, decode_count)
    index = jnp.arange(slots)
    before = (key[None, :] < key[:, None]) | (
        (key[None, :] == key[:, None]) & (index[None, :] < index[:, None])
    )
    position = jnp.sum(before, axis=1)
    order = jnp.sum(
        jnp.where(position[None, :] == index[:, None], index[None, :], 0), axis=1
    ).astype(jnp.int32)
    start = jnp.sum(key[None, :] < jnp.arange(decode_count + 1)[:, None], axis=1).astype(jnp.int32)
    first_rows = decode_count // 2

    up = contribution(half, 0)
    down = contribution(half, 1)
    up, down, block_latents = lax.optimization_barrier((up, down, block_latents))
    to_up = {s: contribution(s, 1) for s in range(half)}
    to_down = {s: contribution(s, 0) for s in range(1, half)}
    for s in range(half - 1, -1, -1):
        up, down = lax.optimization_barrier((up, down))
        up = lax.ppermute(up, AXIS, ahead)
        down = lax.ppermute(down, AXIS, back)
        if s == half - 1:
            up, down, to_up, to_down = lax.optimization_barrier((up, down, to_up, to_down))
        else:
            up, down = lax.optimization_barrier((up, down))
        if s == 0:
            break
        up = up.astype(jnp.float32)
        down = down.astype(jnp.float32)
        if s == half - 1:
            up = jnp.pad(up, ((0, row_count - split), (0, 0)))
            down = jnp.pad(down, ((split, 0), (0, 0)))
        up = (up + to_up[s].astype(jnp.float32)).astype(jnp.bfloat16)
        down = (down + to_down[s].astype(jnp.float32)).astype(jnp.bfloat16)
        if s == 1:
            early = attend(
                order, start, slot_length, queries, own_latent, block_latents, 0, first_rows
            )
            up, down, early = lax.optimization_barrier((up, down, early))
            late = attend(
                order,
                start,
                slot_length,
                queries,
                own_latent,
                block_latents,
                first_rows,
                decode_count - first_rows,
            )
            context = jnp.concatenate([early, late], axis=0)

    def finish(lo, hi):
        total = up[lo:hi].astype(jnp.float32) + down[lo:hi].astype(jnp.float32)
        return (total + to_up[0][lo:hi].astype(jnp.float32)).astype(jnp.bfloat16)

    return (finish(0, split), finish(split, row_count), context)


def solution(mesh):
    rows = P(("groups", "expert"), None)
    blocks = P(("groups", "expert"), None, None)
    line = P(("groups", "expert"))
    weights = P("expert", None, None)
    return jax.shard_map(
        per_device,
        mesh=mesh,
        in_specs=(rows,) * 6 + (weights, weights, blocks, rows, blocks, line, line, line),
        out_specs=(rows, rows, blocks),
        check_vma=False,
    )
```

```python
import functools

import jax
import jax.numpy as jnp
import numpy as np
from jax import lax
from jax.experimental import pallas as pl
from jax.experimental.pallas import tpu as pltpu
from jax.sharding import PartitionSpec as P

KV = 512
CAPC = 2

softmax_scale = 192.0 ** (-0.5)
gate_unit = 65536.0
AXIS = "expert"
VMEM_LIMIT = 16 << 20


def mlp_kernel(sizes, tile, *refs):
    count = len(sizes)
    x_refs = refs[:count]
    up_hbm, down_hbm, mine_hbm, other_hbm = refs[count : count + 4]
    rows_ref, up_ref, down_ref, part_ref, x_sems, up_sems, down_sems, out_sems = refs[count + 4 :]
    width = up_hbm.shape[0]
    half = down_hbm.shape[0]
    tiles = width // tile
    size = mine_hbm.shape[0]
    spans = [pl.ds(k * tile, tile) for k in range(tiles)]
    starts = [sum(sizes[:c]) for c in range(count)]
    x_copies = [
        [
            pltpu.make_async_copy(
                x_refs[c].at[:, spans[k]],
                rows_ref.at[pl.ds(starts[c], sizes[c]), spans[k]],
                x_sems.at[c, k],
            )
            for c in range(count)
        ]
        for k in range(tiles)
    ]
    up_copies = [
        pltpu.make_async_copy(up_hbm.at[s], up_ref.at[s], up_sems.at[k])
        for k, s in enumerate(spans)
    ]
    down_copies = [
        pltpu.make_async_copy(down_hbm.at[:, s], down_ref.at[:, s], down_sems.at[k])
        for k, s in enumerate(spans)
    ]
    for k in range(tiles):
        for copy in x_copies[k]:
            copy.start()
        up_copies[k].start()
    for copy in down_copies:
        copy.start()
    merged = None
    for k in range(tiles):
        for copy in x_copies[k]:
            copy.wait()
        up_copies[k].wait()
        cols = slice(k * tile, (k + 1) * tile)
        part = jnp.dot(rows_ref[:, cols], up_ref[cols, :], preferred_element_type=jnp.float32)
        merged = part if merged is None else merged + part
    hidden = (jax.nn.silu(merged[:, :half]) * merged[:, half:]).astype(jnp.bfloat16)
    out_copies = []
    for n, s in enumerate(spans):
        down_copies[n].wait()
        cols = slice(n * tile, (n + 1) * tile)
        part = jnp.dot(hidden, down_ref[:, cols], preferred_element_type=jnp.float32)
        part_ref[:, cols] = part.astype(jnp.bfloat16)
        for c, target in enumerate((mine_hbm, other_hbm)):
            copy = pltpu.make_async_copy(
                part_ref.at[pl.ds(c * size, size), s], target.at[:, s], out_sems.at[c, n]
            )
            copy.start()
            out_copies.append(copy)
    for copy in out_copies:
        copy.wait()


def mlp(mine, other, gate_up, down_proj, tile=1024):
    chunks = mine + other
    width, both = gate_up.shape
    half = down_proj.shape[0]
    tile = tile if width % tile == 0 else width
    tiles = width // tile
    sizes = tuple(c.shape[0] for c in chunks)
    rows = sum(sizes)
    anywhere = pl.BlockSpec(memory_space=pltpu.HBM)
    dma = pltpu.SemaphoreType.DMA
    return pl.pallas_call(
        functools.partial(mlp_kernel, sizes, tile),
        in_specs=[anywhere] * (len(chunks) + 2),
        out_specs=[anywhere, anywhere],
        out_shape=[jax.ShapeDtypeStruct((rows // 2, width), jnp.bfloat16)] * 2,
        scratch_shapes=[
            pltpu.VMEM((rows, width), jnp.bfloat16),
            pltpu.VMEM((width, both), jnp.bfloat16),
            pltpu.VMEM((half, width), jnp.bfloat16),
            pltpu.VMEM((rows, width), jnp.bfloat16),
            dma((len(chunks), tiles)),
            dma((tiles,)),
            dma((tiles,)),
            dma((2, tiles)),
        ],
        compiler_params=pltpu.CompilerParams(vmem_limit_bytes=44 << 20),
        cost_estimate=pl.CostEstimate(
            flops=6 * rows * width * half,
            bytes_accessed=6 * width * half + 4 * rows * width,
            transcendentals=rows * half,
        ),
        name="mlp",
    )(*chunks, gate_up, down_proj)


def ship_kernel(source_ref, block_ref, out_ref):
    for i in range(out_ref.shape[0]):
        out_ref[i] = block_ref[source_ref[i]]


def ship_blocks(latents, source):
    slots = source.shape[0]
    resident = pl.BlockSpec(memory_space=pltpu.VMEM)
    return pl.pallas_call(
        ship_kernel,
        in_specs=[pl.BlockSpec(memory_space=pltpu.SMEM), resident],
        out_specs=resident,
        out_shape=jax.ShapeDtypeStruct((slots,) + latents.shape[1:], latents.dtype),
        compiler_params=pltpu.CompilerParams(vmem_limit_bytes=16 << 20),
        cost_estimate=pl.CostEstimate(
            flops=0, bytes_accessed=6 * latents.size, transcendentals=0
        ),
        name="ship",
    )(source, latents)


def attend_kernel(order_ref, start_ref, length_ref, query_ref, own_ref, latent_ref, out_ref):
    row = pl.program_id(0)
    query = query_ref[0]
    own = own_ref[0].astype(jnp.float32)
    own_score = (
        jnp.sum(query.astype(jnp.float32) * own, axis=1, keepdims=True) * softmax_scale
    )
    heads = query.shape[0]
    block = latent_ref.shape[1]

    def step(j, state):
        top, total, value = state
        slot = order_ref[j]
        latent = latent_ref[slot]
        scores = (
            lax.dot_general(
                query, latent, (((1,), (1,)), ((), ())), preferred_element_type=jnp.float32
            )
            * softmax_scale
        )
        inside = lax.broadcasted_iota(jnp.int32, (heads, block), 1) < length_ref[slot]
        span_max = jnp.max(jnp.where(inside, scores, -jnp.inf), axis=1, keepdims=True)
        weights = jnp.where(inside, jnp.exp(scores - span_max), 0.0)
        span_total = jnp.sum(weights, axis=1, keepdims=True)
        span_value = jnp.dot(
            weights.astype(jnp.bfloat16), latent[:, :KV], preferred_element_type=jnp.float32
        )
        higher = jnp.maximum(top, span_max)
        old = jnp.exp(top - higher)
        new = jnp.exp(span_max - higher)
        return (higher, old * total + new * span_total, old * value + new * span_value)

    state = (
        own_score,
        jnp.ones((heads, 1), jnp.float32),
        jnp.broadcast_to(own[:, :KV], (heads, KV)),
    )
    top, total, value = lax.fori_loop(start_ref[row], start_ref[row + 1], step, state)
    out_ref[0] = (value / total).astype(jnp.bfloat16)


def attend(order, start, lengths, queries, own_latent, latents, first, rows):
    _, heads, width = queries.shape
    slots, block, _ = latents.shape
    own_latent = own_latent.reshape(own_latent.shape[0], 1, width)
    return pl.pallas_call(
        attend_kernel,
        grid_spec=pltpu.PrefetchScalarGridSpec(
            num_scalar_prefetch=3,
            grid=(rows,),
            in_specs=[
                pl.BlockSpec((1, heads, width), lambda i, *_: (i + first, 0, 0)),
                pl.BlockSpec((1, 1, width), lambda i, *_: (i + first, 0, 0)),
                pl.BlockSpec((slots, block, width), lambda i, *_: (0, 0, 0)),
            ],
            out_specs=pl.BlockSpec((1, heads, KV), lambda i, *_: (i, 0, 0)),
        ),
        out_shape=jax.ShapeDtypeStruct((rows, heads, KV), jnp.bfloat16),
        compiler_params=pltpu.CompilerParams(vmem_limit_bytes=VMEM_LIMIT),
        cost_estimate=pl.CostEstimate(
            flops=2 * slots * heads * block * width,
            bytes_accessed=2 * (rows * heads * (width + KV) + slots * block * width),
            transcendentals=slots * heads * block,
        ),
        name="attend",
    )(order, start[first : first + rows + 1], lengths, queries, own_latent, latents)


def dense_gates(experts, gates, expert_count):
    named = experts[:, :, None] == jnp.arange(expert_count)[None, None, :]
    return jnp.sum(jnp.where(named, gates[:, :, None], 0), axis=1)


def per_device(
    prefill_tokens,
    prefill_experts,
    prefill_gates,
    decode_rows,
    decode_experts,
    decode_gates,
    w_gate_up,
    w_down,
    queries,
    own_latent,
    latents,
    span_owner,
    span_request,
    span_length,
):
    devices = lax.axis_size(AXIS)
    chips = devices // 2
    half = chips // 2
    gate_up = w_gate_up[0]
    down_proj = w_down[0]
    prefill_count = prefill_tokens.shape[0]
    decode_count = decode_rows.shape[0]
    row_count = prefill_count + decode_count
    split = prefill_count

    ring = list(range(0, chips, 2)) + list(range(1, chips, 2))[::-1]
    place_of = np.zeros(chips, np.int32)
    for i, chip in enumerate(ring):
        place_of[chip] = i
    ahead = [
        (2 * ring[i] + c, 2 * ring[(i + 1) % chips] + c) for i in range(chips) for c in range(2)
    ]
    back = [(b, a) for a, b in ahead]
    across = [(i, i ^ 1) for i in range(devices)]
    me = lax.axis_index(AXIS)
    neighbours = np.zeros((devices, chips), np.int32)
    for device in range(devices):
        for shift in range(chips):
            chip = ring[(place_of[device // 2] + shift) % chips]
            neighbours[device, shift] = 2 * chip + device % 2

    span_count = span_owner.shape[0]
    block_rows = latents.shape[1]
    slots = devices * CAPC
    numbered = jnp.arange(span_count)
    earlier = (span_owner[None, :] == span_owner[:, None]) & (numbered[None, :] < numbered[:, None])
    span_rank = jnp.sum(earlier, axis=1)
    slot_of = span_owner * CAPC + span_rank
    placed = slot_of[None, :] == jnp.arange(slots)[:, None]
    source = jnp.sum(jnp.where(placed, numbered[None, :], 0), axis=1).astype(jnp.int32)
    codes = span_request * (block_rows + 1) + span_length
    slot_codes = jnp.sum(jnp.where(placed, codes[None, :], 0), axis=1).astype(jnp.int32)

    gates = jnp.concatenate(
        [
            dense_gates(prefill_experts, prefill_gates, chips),
            dense_gates(decode_experts, decode_gates, chips),
        ],
        axis=0,
    )
    small = jnp.concatenate(
        [jnp.repeat(gates.T, 2, axis=0), slot_codes.reshape(devices, CAPC)], axis=1
    ).astype(jnp.int32)
    small = lax.all_to_all(small, AXIS, split_axis=0, concat_axis=0, tiled=True)
    shipped = ship_blocks(latents, source)

    own = [prefill_tokens, decode_rows]
    sizes = [prefill_count, decode_count]
    front = {1: [lax.ppermute(c, AXIS, ahead) for c in own]}
    rear = {1: [lax.ppermute(c, AXIS, back) for c in own]}
    front[1][0], rear[1][0], shipped, small = lax.optimization_barrier(
        (front[1][0], rear[1][0], shipped, small)
    )
    at_shift = lax.dynamic_index_in_dim(jnp.asarray(neighbours), me, 0, keepdims=False)
    picked = at_shift[:, None] == jnp.arange(devices)[None, :]
    shift_gates = jnp.sum(jnp.where(picked[:, :, None], small[None, :, :row_count], 0), axis=1)
    shift_gates = shift_gates.astype(jnp.float32) / gate_unit
    slot_codes = small[:, row_count:].reshape(-1)
    slot_length = slot_codes % (block_rows + 1)
    slot_request = slot_codes // (block_rows + 1)

    for s in range(2, half):
        front[s] = [lax.ppermute(c, AXIS, ahead) for c in front[s - 1]]
        rear[s] = [lax.ppermute(c, AXIS, back) for c in rear[s - 1]]

    def work(s, mine):
        other = [lax.ppermute(c, AXIS, across) for c in mine]
        return mlp(mine, other, gate_up, down_proj)

    first = min(2, half - 1)
    near, _ = lax.optimization_barrier((front[1] + rear[1] + own, front[first][:1]))
    results = {1: work(1, near)}
    last_rear, results[1] = lax.optimization_barrier((rear[half - 1][1], results[1]))
    front[half] = [lax.ppermute(front[half - 1][0], AXIS, ahead)]
    rear[half] = [lax.ppermute(last_rear, AXIS, back)]
    front, rear, shipped, shift_gates, results = lax.optimization_barrier(
        (front, rear, shipped, shift_gates, results)
    )
    block_latents = lax.all_to_all(shipped, AXIS, split_axis=0, concat_axis=0, tiled=True)
    for s in [half] + list(range(half - 1, 1, -1)):
        results[s] = work(s, front[s] + rear[s])
    parts = {s: (part, lax.ppermute(rest, AXIS, across)) for s, (part, rest) in results.items()}

    def contribution(s, k, flow):
        part, from_other = parts[max(s, 1)]
        size = sizes[flow]
        lo = flow * split
        if s == half:
            lo = k * split
        elif s == 0:
            lo = lo + 2 * row_count
        else:
            lo = lo + k * row_count
        both = part[lo : lo + size].astype(jnp.float32) + from_other[lo : lo + size].astype(
            jnp.float32
        )
        weight = shift_gates[((-s, s)[k] + chips) % chips, flow * split : flow * split + size]
        return (weight[:, None] * both).astype(jnp.bfloat16)

    key = jnp.where(slot_length > 0, slot_request, decode_count)
    index = jnp.arange(slots)
    before = (key[None, :] < key[:, None]) | (
        (key[None, :] == key[:, None]) & (index[None, :] < index[:, None])
    )
    position = jnp.sum(before, axis=1)
    order = jnp.sum(
        jnp.where(position[None, :] == index[:, None], index[None, :], 0), axis=1
    ).astype(jnp.int32)
    start = jnp.sum(key[None, :] < jnp.arange(decode_count + 1)[:, None], axis=1).astype(jnp.int32)
    first_rows = decode_count // 2

    sums = [{"up": contribution(half, 0, 0)}, {"down": contribution(half, 1, 1)}]
    sums, block_latents = lax.optimization_barrier((sums, block_latents))
    terms = {
        (s, flow): {"up": contribution(s, 1, flow), "down": contribution(s, 0, flow)}
        for s in range(1, half)
        for flow in range(2)
    }
    last = [contribution(0, 0, flow) for flow in range(2)]
    course = {"up": ahead, "down": back}

    def add(a, b):
        return (a.astype(jnp.float32) + b.astype(jnp.float32)).astype(jnp.bfloat16)

    for s in range(half - 1, -1, -1):
        for flow in range(2):
            moved = {
                way: lax.ppermute(value, AXIS, course[way]) for way, value in sums[flow].items()
            }
            if s == half - 1:
                moved, terms, last = lax.optimization_barrier((moved, terms, last))
            else:
                moved = lax.optimization_barrier(moved)
            if s == 0:
                sums[flow] = moved
                continue
            added = {
                way: add(moved[way], term) if way in moved else term
                for way, term in terms[(s, flow)].items()
            }
            if s == 1 and flow == 0:
                early = attend(
                    order, start, slot_length, queries, own_latent, block_latents, 0, first_rows
                )
            if s == 1 and flow == 1:
                added, early = lax.optimization_barrier((added, early))
                late = attend(
                    order,
                    start,
                    slot_length,
                    queries,
                    own_latent,
                    block_latents,
                    first_rows,
                    decode_count - first_rows,
                )
                context = jnp.concatenate([early, late], axis=0)
            sums[flow] = lax.optimization_barrier(added)

    def finish(flow):
        total = sums[flow]["up"].astype(jnp.float32) + sums[flow]["down"].astype(jnp.float32)
        return (total + last[flow].astype(jnp.float32)).astype(jnp.bfloat16)

    return (finish(0), finish(1), context)


def solution(mesh):
    rows = P(("groups", "expert"), None)
    blocks = P(("groups", "expert"), None, None)
    line = P(("groups", "expert"))
    weights = P("expert", None, None)
    return jax.shard_map(
        per_device,
        mesh=mesh,
        in_specs=(rows,) * 6 + (weights, weights, blocks, rows, blocks, line, line, line),
        out_specs=(rows, rows, blocks),
        check_vma=False,
    )
```

```python
import functools

import jax
import jax.numpy as jnp
import numpy as np
from jax import lax
from jax.experimental import pallas as pl
from jax.experimental.pallas import tpu as pltpu
from jax.sharding import PartitionSpec as P

KV = 512
CAPC = 2

softmax_scale = 192.0 ** (-0.5)
gate_unit = 65536.0
AXIS = "expert"
VMEM_LIMIT = 16 << 20


def mlp_kernel(sizes, tile, *refs):
    count = len(sizes)
    x_refs = refs[:count]
    up_hbm, down_hbm, mine_hbm, other_hbm = refs[count : count + 4]
    rows_ref, up_ref, down_ref, part_ref, x_sems, up_sems, down_sems, out_sems = refs[count + 4 :]
    width = up_hbm.shape[0]
    half = down_hbm.shape[0]
    tiles = width // tile
    size = mine_hbm.shape[0]
    spans = [pl.ds(k * tile, tile) for k in range(tiles)]
    starts = [sum(sizes[:c]) for c in range(count)]
    x_copies = [
        [
            pltpu.make_async_copy(
                x_refs[c].at[:, spans[k]],
                rows_ref.at[pl.ds(starts[c], sizes[c]), spans[k]],
                x_sems.at[c, k],
            )
            for c in range(count)
        ]
        for k in range(tiles)
    ]
    up_copies = [
        pltpu.make_async_copy(up_hbm.at[s], up_ref.at[s], up_sems.at[k])
        for k, s in enumerate(spans)
    ]
    down_copies = [
        pltpu.make_async_copy(down_hbm.at[:, s], down_ref.at[:, s], down_sems.at[k])
        for k, s in enumerate(spans)
    ]
    for k in range(tiles):
        for copy in x_copies[k]:
            copy.start()
        up_copies[k].start()
    for copy in down_copies:
        copy.start()
    merged = None
    for k in range(tiles):
        for copy in x_copies[k]:
            copy.wait()
        up_copies[k].wait()
        cols = slice(k * tile, (k + 1) * tile)
        part = jnp.dot(rows_ref[:, cols], up_ref[cols, :], preferred_element_type=jnp.float32)
        merged = part if merged is None else merged + part
    hidden = (jax.nn.silu(merged[:, :half]) * merged[:, half:]).astype(jnp.bfloat16)
    out_copies = []
    for n, s in enumerate(spans):
        down_copies[n].wait()
        cols = slice(n * tile, (n + 1) * tile)
        part = jnp.dot(hidden, down_ref[:, cols], preferred_element_type=jnp.float32)
        part_ref[:, cols] = part.astype(jnp.bfloat16)
        for c, target in enumerate((mine_hbm, other_hbm)):
            copy = pltpu.make_async_copy(
                part_ref.at[pl.ds(c * size, size), s], target.at[:, s], out_sems.at[c, n]
            )
            copy.start()
            out_copies.append(copy)
    for copy in out_copies:
        copy.wait()


def mlp(mine, other, gate_up, down_proj, tile=1024):
    chunks = mine + other
    width, both = gate_up.shape
    half = down_proj.shape[0]
    tile = tile if width % tile == 0 else width
    tiles = width // tile
    sizes = tuple(c.shape[0] for c in chunks)
    rows = sum(sizes)
    anywhere = pl.BlockSpec(memory_space=pl.ANY)
    dma = pltpu.SemaphoreType.DMA
    return pl.pallas_call(
        functools.partial(mlp_kernel, sizes, tile),
        in_specs=[anywhere] * len(chunks) + [pl.BlockSpec(memory_space=pltpu.HBM)] * 2,
        out_specs=[anywhere, anywhere],
        out_shape=[jax.ShapeDtypeStruct((rows // 2, width), jnp.bfloat16)] * 2,
        scratch_shapes=[
            pltpu.VMEM((rows, width), jnp.bfloat16),
            pltpu.VMEM((width, both), jnp.bfloat16),
            pltpu.VMEM((half, width), jnp.bfloat16),
            pltpu.VMEM((rows, width), jnp.bfloat16),
            dma((len(chunks), tiles)),
            dma((tiles,)),
            dma((tiles,)),
            dma((2, tiles)),
        ],
        compiler_params=pltpu.CompilerParams(vmem_limit_bytes=44 << 20),
        cost_estimate=pl.CostEstimate(
            flops=6 * rows * width * half,
            bytes_accessed=6 * width * half + 4 * rows * width,
            transcendentals=rows * half,
        ),
        name="mlp",
    )(*chunks, gate_up, down_proj)


def ship_kernel(source_ref, block_ref, out_ref):
    for i in range(out_ref.shape[0]):
        out_ref[i] = block_ref[source_ref[i]]


def ship_blocks(latents, source):
    slots = source.shape[0]
    resident = pl.BlockSpec(memory_space=pltpu.VMEM)
    return pl.pallas_call(
        ship_kernel,
        in_specs=[pl.BlockSpec(memory_space=pltpu.SMEM), resident],
        out_specs=resident,
        out_shape=jax.ShapeDtypeStruct((slots,) + latents.shape[1:], latents.dtype),
        compiler_params=pltpu.CompilerParams(vmem_limit_bytes=16 << 20),
        cost_estimate=pl.CostEstimate(
            flops=0, bytes_accessed=6 * latents.size, transcendentals=0
        ),
        name="ship",
    )(source, latents)


def attend_kernel(order_ref, start_ref, length_ref, query_ref, own_ref, latent_ref, out_ref):
    row = pl.program_id(0)
    query = query_ref[0]
    own = own_ref[0].astype(jnp.float32)
    own_score = (
        jnp.sum(query.astype(jnp.float32) * own, axis=1, keepdims=True) * softmax_scale
    )
    heads = query.shape[0]
    block = latent_ref.shape[1]

    def step(j, state):
        top, total, value = state
        slot = order_ref[j]
        latent = latent_ref[slot]
        scores = (
            lax.dot_general(
                query, latent, (((1,), (1,)), ((), ())), preferred_element_type=jnp.float32
            )
            * softmax_scale
        )
        inside = lax.broadcasted_iota(jnp.int32, (heads, block), 1) < length_ref[slot]
        span_max = jnp.max(jnp.where(inside, scores, -jnp.inf), axis=1, keepdims=True)
        weights = jnp.where(inside, jnp.exp(scores - span_max), 0.0)
        span_total = jnp.sum(weights, axis=1, keepdims=True)
        span_value = jnp.dot(
            weights.astype(jnp.bfloat16), latent[:, :KV], preferred_element_type=jnp.float32
        )
        higher = jnp.maximum(top, span_max)
        old = jnp.exp(top - higher)
        new = jnp.exp(span_max - higher)
        return (higher, old * total + new * span_total, old * value + new * span_value)

    state = (
        own_score,
        jnp.ones((heads, 1), jnp.float32),
        jnp.broadcast_to(own[:, :KV], (heads, KV)),
    )
    top, total, value = lax.fori_loop(start_ref[row], start_ref[row + 1], step, state)
    out_ref[0] = (value / total).astype(jnp.bfloat16)


def attend(order, start, lengths, queries, own_latent, latents, first, rows):
    _, heads, width = queries.shape
    slots, block, _ = latents.shape
    own_latent = own_latent.reshape(own_latent.shape[0], 1, width)
    return pl.pallas_call(
        attend_kernel,
        grid_spec=pltpu.PrefetchScalarGridSpec(
            num_scalar_prefetch=3,
            grid=(rows,),
            in_specs=[
                pl.BlockSpec((1, heads, width), lambda i, *_: (i + first, 0, 0)),
                pl.BlockSpec((1, 1, width), lambda i, *_: (i + first, 0, 0)),
                pl.BlockSpec((slots, block, width), lambda i, *_: (0, 0, 0)),
            ],
            out_specs=pl.BlockSpec((1, heads, KV), lambda i, *_: (i, 0, 0)),
        ),
        out_shape=jax.ShapeDtypeStruct((rows, heads, KV), jnp.bfloat16),
        compiler_params=pltpu.CompilerParams(vmem_limit_bytes=VMEM_LIMIT),
        cost_estimate=pl.CostEstimate(
            flops=2 * slots * heads * block * width,
            bytes_accessed=2 * (rows * heads * (width + KV) + slots * block * width),
            transcendentals=slots * heads * block,
        ),
        name="attend",
    )(order, start[first : first + rows + 1], lengths, queries, own_latent, latents)


def dense_gates(experts, gates, expert_count):
    named = experts[:, :, None] == jnp.arange(expert_count)[None, None, :]
    return jnp.sum(jnp.where(named, gates[:, :, None], 0), axis=1)


def per_device(
    prefill_tokens,
    prefill_experts,
    prefill_gates,
    decode_rows,
    decode_experts,
    decode_gates,
    w_gate_up,
    w_down,
    queries,
    own_latent,
    latents,
    span_owner,
    span_request,
    span_length,
):
    devices = lax.axis_size(AXIS)
    chips = devices // 2
    half = chips // 2
    gate_up = w_gate_up[0]
    down_proj = w_down[0]
    prefill_count = prefill_tokens.shape[0]
    decode_count = decode_rows.shape[0]
    row_count = prefill_count + decode_count
    split = prefill_count

    ring = list(range(0, chips, 2)) + list(range(1, chips, 2))[::-1]
    place_of = np.zeros(chips, np.int32)
    for i, chip in enumerate(ring):
        place_of[chip] = i
    ahead = [
        (2 * ring[i] + c, 2 * ring[(i + 1) % chips] + c) for i in range(chips) for c in range(2)
    ]
    back = [(b, a) for a, b in ahead]
    across = [(i, i ^ 1) for i in range(devices)]
    me = lax.axis_index(AXIS)
    neighbours = np.zeros((devices, chips), np.int32)
    for device in range(devices):
        for shift in range(chips):
            chip = ring[(place_of[device // 2] + shift) % chips]
            neighbours[device, shift] = 2 * chip + device % 2

    span_count = span_owner.shape[0]
    block_rows = latents.shape[1]
    slots = devices * CAPC
    numbered = jnp.arange(span_count)
    earlier = (span_owner[None, :] == span_owner[:, None]) & (numbered[None, :] < numbered[:, None])
    span_rank = jnp.sum(earlier, axis=1)
    slot_of = span_owner * CAPC + span_rank
    placed = slot_of[None, :] == jnp.arange(slots)[:, None]
    source = jnp.sum(jnp.where(placed, numbered[None, :], 0), axis=1).astype(jnp.int32)
    codes = span_request * (block_rows + 1) + span_length
    slot_codes = jnp.sum(jnp.where(placed, codes[None, :], 0), axis=1).astype(jnp.int32)

    gates = jnp.concatenate(
        [
            dense_gates(prefill_experts, prefill_gates, chips),
            dense_gates(decode_experts, decode_gates, chips),
        ],
        axis=0,
    )
    small = jnp.concatenate(
        [jnp.repeat(gates.T, 2, axis=0), slot_codes.reshape(devices, CAPC)], axis=1
    ).astype(jnp.int32)
    small = lax.all_to_all(small, AXIS, split_axis=0, concat_axis=0, tiled=True)
    shipped = ship_blocks(latents, source)

    own = [prefill_tokens, decode_rows]
    sizes = [prefill_count, decode_count]
    front = {1: [lax.ppermute(c, AXIS, ahead) for c in own]}
    rear = {1: [lax.ppermute(c, AXIS, back) for c in own]}
    front[1][0], rear[1][0], shipped, small = lax.optimization_barrier(
        (front[1][0], rear[1][0], shipped, small)
    )
    at_shift = lax.dynamic_index_in_dim(jnp.asarray(neighbours), me, 0, keepdims=False)
    picked = at_shift[:, None] == jnp.arange(devices)[None, :]
    shift_gates = jnp.sum(jnp.where(picked[:, :, None], small[None, :, :row_count], 0), axis=1)
    shift_gates = shift_gates.astype(jnp.float32) / gate_unit
    slot_codes = small[:, row_count:].reshape(-1)
    slot_length = slot_codes % (block_rows + 1)
    slot_request = slot_codes // (block_rows + 1)

    for s in range(2, half):
        front[s] = [lax.ppermute(c, AXIS, ahead) for c in front[s - 1]]
        rear[s] = [lax.ppermute(c, AXIS, back) for c in rear[s - 1]]

    def work(s, mine):
        other = [lax.ppermute(c, AXIS, across) for c in mine]
        return mlp(mine, other, gate_up, down_proj)

    front[half] = [lax.ppermute(front[half - 1][0], AXIS, ahead)]
    rear[half] = [lax.ppermute(rear[half - 1][1], AXIS, back)]
    front, rear, shipped, shift_gates = lax.optimization_barrier(
        (front, rear, shipped, shift_gates)
    )
    block_latents = lax.all_to_all(shipped, AXIS, split_axis=0, concat_axis=0, tiled=True)
    results = {}
    for s in range(half, 0, -1):
        results[s] = work(s, front[s] + rear[s] + (own if s == 1 else []))
    parts = {s: (part, lax.ppermute(rest, AXIS, across)) for s, (part, rest) in results.items()}

    def contribution(s, k, flow):
        part, from_other = parts[max(s, 1)]
        size = sizes[flow]
        lo = flow * split
        if s == half:
            lo = k * split
        elif s == 0:
            lo = lo + 2 * row_count
        else:
            lo = lo + k * row_count
        both = part[lo : lo + size].astype(jnp.float32) + from_other[lo : lo + size].astype(
            jnp.float32
        )
        weight = shift_gates[((-s, s)[k] + chips) % chips, flow * split : flow * split + size]
        return (weight[:, None] * both).astype(jnp.bfloat16)

    key = jnp.where(slot_length > 0, slot_request, decode_count)
    index = jnp.arange(slots)
    before = (key[None, :] < key[:, None]) | (
        (key[None, :] == key[:, None]) & (index[None, :] < index[:, None])
    )
    position = jnp.sum(before, axis=1)
    order = jnp.sum(
        jnp.where(position[None, :] == index[:, None], index[None, :], 0), axis=1
    ).astype(jnp.int32)
    start = jnp.sum(key[None, :] < jnp.arange(decode_count + 1)[:, None], axis=1).astype(jnp.int32)
    first_rows = decode_count // 2

    sums = [{"up": contribution(half, 0, 0)}, {"down": contribution(half, 1, 1)}]
    terms = {
        (s, flow): {"up": contribution(s, 1, flow), "down": contribution(s, 0, flow)}
        for s in range(1, half)
        for flow in range(2)
    }
    last = [contribution(0, 0, flow) for flow in range(2)]
    course = {"up": ahead, "down": back}

    def add(a, b):
        return (a.astype(jnp.float32) + b.astype(jnp.float32)).astype(jnp.bfloat16)

    for s in range(half - 1, -1, -1):
        for flow in range(2):
            moved = {
                way: lax.ppermute(value, AXIS, course[way]) for way, value in sums[flow].items()
            }
            if s == half - 1:
                moved, terms, last, block_latents = lax.optimization_barrier(
                    (moved, terms, last, block_latents)
                )
            else:
                moved = lax.optimization_barrier(moved)
            if s == 0:
                sums[flow] = moved
                continue
            added = {
                way: add(moved[way], term) if way in moved else term
                for way, term in terms[(s, flow)].items()
            }
            if s == 1 and flow == 0:
                early = attend(
                    order, start, slot_length, queries, own_latent, block_latents, 0, first_rows
                )
            if s == 1 and flow == 1:
                added, early = lax.optimization_barrier((added, early))
                late = attend(
                    order,
                    start,
                    slot_length,
                    queries,
                    own_latent,
                    block_latents,
                    first_rows,
                    decode_count - first_rows,
                )
                context = jnp.concatenate([early, late], axis=0)
            sums[flow] = lax.optimization_barrier(added)

    def finish(flow):
        total = sums[flow]["up"].astype(jnp.float32) + sums[flow]["down"].astype(jnp.float32)
        return (total + last[flow].astype(jnp.float32)).astype(jnp.bfloat16)

    return (finish(0), finish(1), context)


def solution(mesh):
    rows = P(("groups", "expert"), None)
    blocks = P(("groups", "expert"), None, None)
    line = P(("groups", "expert"))
    weights = P("expert", None, None)
    return jax.shard_map(
        per_device,
        mesh=mesh,
        in_specs=(rows,) * 6 + (weights, weights, blocks, rows, blocks, line, line, line),
        out_specs=(rows, rows, blocks),
        check_vma=False,
    )
```

```python
import functools

import jax
import jax.numpy as jnp
import numpy as np
from jax import lax
from jax.experimental import pallas as pl
from jax.experimental.pallas import tpu as pltpu
from jax.sharding import PartitionSpec as P

KV = 512
CAPC = 2

softmax_scale = 192.0 ** (-0.5)
gate_unit = 65536.0
AXIS = "expert"
VMEM_LIMIT = 16 << 20


def mlp_kernel(blocks, tile, *refs):
    count = sum(len(sizes) for sizes in blocks)
    total = len(blocks)
    x_refs = refs[:count]
    up_hbm, down_hbm = refs[count : count + 2]
    out_refs = refs[count + 2 : count + 2 + 2 * total]
    rows_ref, up_ref, down_ref, part_ref, merged_ref, hidden_ref = refs[
        count + 2 + 2 * total : count + 8 + 2 * total
    ]
    x_sems, up_sems, down_sems, out_sems = refs[count + 8 + 2 * total :]
    width = up_hbm.shape[0]
    half = down_hbm.shape[0]
    tiles = width // tile
    x_copies = []
    at = 0
    for b, sizes in enumerate(blocks):
        copies = []
        row = 0
        for size in sizes:
            copies.append(
                pltpu.make_async_copy(
                    x_refs[at], rows_ref.at[b % 2, pl.ds(row, size)], x_sems.at[at]
                )
            )
            row += size
            at += 1
        x_copies.append(copies)
    def up_copy(k):
        span = pl.ds(pl.multiple_of(k * tile, tile), tile)
        return pltpu.make_async_copy(up_hbm.at[span], up_ref.at[span], up_sems.at[k])

    def down_copy(k):
        span = pl.ds(pl.multiple_of(k * tile, tile), tile)
        return pltpu.make_async_copy(down_hbm.at[:, span], down_ref.at[:, span], down_sems.at[k])

    for copy in x_copies[0]:
        copy.start()
    for k in range(tiles):
        up_copy(k).start()
    for k in range(tiles):
        down_copy(k).start()
    out_copies = []
    for b, sizes in enumerate(blocks):
        slot = b % 2
        rows = sum(sizes)
        if b + 1 < total:
            for copy in x_copies[b + 1]:
                copy.start()
        for copy in x_copies[b]:
            copy.wait()
        merged_ref[:rows] = jnp.zeros((rows, 2 * half), jnp.float32)

        def up_step(k, _, b=b, slot=slot, rows=rows):
            if b == 0:
                up_copy(k).wait()
            span = pl.ds(pl.multiple_of(k * tile, tile), tile)
            merged_ref[:rows] += jnp.dot(
                rows_ref[slot, :rows, span], up_ref[span, :], preferred_element_type=jnp.float32
            )
            return 0

        lax.fori_loop(0, tiles, up_step, 0)
        merged = merged_ref[:rows]
        hidden_ref[:rows] = (jax.nn.silu(merged[:, :half]) * merged[:, half:]).astype(jnp.bfloat16)
        if b >= 2:
            for copy in out_copies[b - 2]:
                copy.wait()

        def down_step(k, _, b=b, slot=slot, rows=rows):
            if b == 0:
                down_copy(k).wait()
            span = pl.ds(pl.multiple_of(k * tile, tile), tile)
            part = jnp.dot(
                hidden_ref[:rows], down_ref[:, span], preferred_element_type=jnp.float32
            )
            part_ref[slot, :rows, span] = part.astype(jnp.bfloat16)
            return 0

        lax.fori_loop(0, tiles, down_step, 0)
        size = rows // 2
        copies = []
        for c in range(2):
            copy = pltpu.make_async_copy(
                part_ref.at[slot, pl.ds(c * size, size)], out_refs[2 * b + c], out_sems.at[b, c]
            )
            copy.start()
            copies.append(copy)
        out_copies.append(copies)
    for copies in out_copies[-2:]:
        for copy in copies:
            copy.wait()


def mlp(blocks, gate_up, down_proj):
    width, both = gate_up.shape
    half = down_proj.shape[0]
    tile = width // 4 if width % 512 == 0 else width
    tiles = width // tile
    sizes = tuple(tuple(c.shape[0] for c in chunks) for chunks in blocks)
    counts = [sum(block) for block in sizes]
    chunks = [c for block in blocks for c in block]
    rows = sum(counts)
    anywhere = pl.BlockSpec(memory_space=pl.ANY)
    dma = pltpu.SemaphoreType.DMA
    results = pl.pallas_call(
        functools.partial(mlp_kernel, sizes, tile),
        in_specs=[anywhere] * len(chunks) + [pl.BlockSpec(memory_space=pltpu.HBM)] * 2,
        out_specs=[anywhere] * (2 * len(blocks)),
        out_shape=[
            jax.ShapeDtypeStruct((n // 2, width), jnp.bfloat16) for n in counts for _ in range(2)
        ],
        scratch_shapes=[
            pltpu.VMEM((2, max(counts), width), jnp.bfloat16),
            pltpu.VMEM((width, both), jnp.bfloat16),
            pltpu.VMEM((half, width), jnp.bfloat16),
            pltpu.VMEM((2, max(counts), width), jnp.bfloat16),
            pltpu.VMEM((max(counts), both), jnp.float32),
            pltpu.VMEM((max(counts), half), jnp.bfloat16),
            dma((len(chunks),)),
            dma((tiles,)),
            dma((tiles,)),
            dma((len(blocks), 2)),
        ],
        compiler_params=pltpu.CompilerParams(vmem_limit_bytes=46 << 20),
        cost_estimate=pl.CostEstimate(
            flops=6 * rows * width * half,
            bytes_accessed=6 * width * half + 4 * rows * width,
            transcendentals=rows * half,
        ),
        name="mlp",
    )(*chunks, gate_up, down_proj)
    return [(results[2 * b], results[2 * b + 1]) for b in range(len(blocks))]


def ship_kernel(source_ref, block_ref, out_ref):
    for i in range(out_ref.shape[0]):
        out_ref[i] = block_ref[source_ref[i]]


def ship_blocks(latents, source):
    slots = source.shape[0]
    resident = pl.BlockSpec(memory_space=pltpu.VMEM)
    return pl.pallas_call(
        ship_kernel,
        in_specs=[pl.BlockSpec(memory_space=pltpu.SMEM), resident],
        out_specs=resident,
        out_shape=jax.ShapeDtypeStruct((slots,) + latents.shape[1:], latents.dtype),
        compiler_params=pltpu.CompilerParams(vmem_limit_bytes=16 << 20),
        cost_estimate=pl.CostEstimate(
            flops=0, bytes_accessed=6 * latents.size, transcendentals=0
        ),
        name="ship",
    )(source, latents)


def attend_kernel(order_ref, start_ref, length_ref, query_ref, own_ref, latent_ref, out_ref):
    row = pl.program_id(0)
    query = query_ref[0]
    own = own_ref[0].astype(jnp.float32)
    own_score = (
        jnp.sum(query.astype(jnp.float32) * own, axis=1, keepdims=True) * softmax_scale
    )
    heads = query.shape[0]
    block = latent_ref.shape[1]

    def step(j, state):
        top, total, value = state
        slot = order_ref[j]
        latent = latent_ref[slot]
        scores = (
            lax.dot_general(
                query, latent, (((1,), (1,)), ((), ())), preferred_element_type=jnp.float32
            )
            * softmax_scale
        )
        inside = lax.broadcasted_iota(jnp.int32, (heads, block), 1) < length_ref[slot]
        span_max = jnp.max(jnp.where(inside, scores, -jnp.inf), axis=1, keepdims=True)
        weights = jnp.where(inside, jnp.exp(scores - span_max), 0.0)
        span_total = jnp.sum(weights, axis=1, keepdims=True)
        span_value = jnp.dot(
            weights.astype(jnp.bfloat16), latent[:, :KV], preferred_element_type=jnp.float32
        )
        higher = jnp.maximum(top, span_max)
        old = jnp.exp(top - higher)
        new = jnp.exp(span_max - higher)
        return (higher, old * total + new * span_total, old * value + new * span_value)

    state = (
        own_score,
        jnp.ones((heads, 1), jnp.float32),
        jnp.broadcast_to(own[:, :KV], (heads, KV)),
    )
    top, total, value = lax.fori_loop(start_ref[row], start_ref[row + 1], step, state)
    out_ref[0] = (value / total).astype(jnp.bfloat16)


def attend(order, start, lengths, queries, own_latent, latents, first, rows):
    _, heads, width = queries.shape
    slots, block, _ = latents.shape
    own_latent = own_latent.reshape(own_latent.shape[0], 1, width)
    return pl.pallas_call(
        attend_kernel,
        grid_spec=pltpu.PrefetchScalarGridSpec(
            num_scalar_prefetch=3,
            grid=(rows,),
            in_specs=[
                pl.BlockSpec((1, heads, width), lambda i, *_: (i + first, 0, 0)),
                pl.BlockSpec((1, 1, width), lambda i, *_: (i + first, 0, 0)),
                pl.BlockSpec((slots, block, width), lambda i, *_: (0, 0, 0)),
            ],
            out_specs=pl.BlockSpec((1, heads, KV), lambda i, *_: (i, 0, 0)),
        ),
        out_shape=jax.ShapeDtypeStruct((rows, heads, KV), jnp.bfloat16),
        compiler_params=pltpu.CompilerParams(vmem_limit_bytes=VMEM_LIMIT),
        cost_estimate=pl.CostEstimate(
            flops=2 * slots * heads * block * width,
            bytes_accessed=2 * (rows * heads * (width + KV) + slots * block * width),
            transcendentals=slots * heads * block,
        ),
        name="attend",
    )(order, start[first : first + rows + 1], lengths, queries, own_latent, latents)


def dense_gates(experts, gates, expert_count):
    named = experts[:, :, None] == jnp.arange(expert_count)[None, None, :]
    return jnp.sum(jnp.where(named, gates[:, :, None], 0), axis=1)


def per_device(
    prefill_tokens,
    prefill_experts,
    prefill_gates,
    decode_rows,
    decode_experts,
    decode_gates,
    w_gate_up,
    w_down,
    queries,
    own_latent,
    latents,
    span_owner,
    span_request,
    span_length,
):
    devices = lax.axis_size(AXIS)
    chips = devices // 2
    half = chips // 2
    gate_up = w_gate_up[0]
    down_proj = w_down[0]
    prefill_count = prefill_tokens.shape[0]
    decode_count = decode_rows.shape[0]
    row_count = prefill_count + decode_count
    split = prefill_count

    ring = list(range(0, chips, 2)) + list(range(1, chips, 2))[::-1]
    place_of = np.zeros(chips, np.int32)
    for i, chip in enumerate(ring):
        place_of[chip] = i
    ahead = [
        (2 * ring[i] + c, 2 * ring[(i + 1) % chips] + c) for i in range(chips) for c in range(2)
    ]
    back = [(b, a) for a, b in ahead]
    across = [(i, i ^ 1) for i in range(devices)]
    me = lax.axis_index(AXIS)
    neighbours = np.zeros((devices, chips), np.int32)
    for device in range(devices):
        for shift in range(chips):
            chip = ring[(place_of[device // 2] + shift) % chips]
            neighbours[device, shift] = 2 * chip + device % 2

    span_count = span_owner.shape[0]
    block_rows = latents.shape[1]
    slots = devices * CAPC
    numbered = jnp.arange(span_count)
    earlier = (span_owner[None, :] == span_owner[:, None]) & (numbered[None, :] < numbered[:, None])
    span_rank = jnp.sum(earlier, axis=1)
    slot_of = span_owner * CAPC + span_rank
    placed = slot_of[None, :] == jnp.arange(slots)[:, None]
    source = jnp.sum(jnp.where(placed, numbered[None, :], 0), axis=1).astype(jnp.int32)
    codes = span_request * (block_rows + 1) + span_length
    slot_codes = jnp.sum(jnp.where(placed, codes[None, :], 0), axis=1).astype(jnp.int32)

    gates = jnp.concatenate(
        [
            dense_gates(prefill_experts, prefill_gates, chips),
            dense_gates(decode_experts, decode_gates, chips),
        ],
        axis=0,
    )
    small = jnp.concatenate(
        [jnp.repeat(gates.T, 2, axis=0), slot_codes.reshape(devices, CAPC)], axis=1
    ).astype(jnp.int32)
    small = lax.all_to_all(small, AXIS, split_axis=0, concat_axis=0, tiled=True)
    shipped = ship_blocks(latents, source)

    own = [prefill_tokens, decode_rows]
    sizes = [prefill_count, decode_count]
    mine = {0: own}
    front = [lax.ppermute(c, AXIS, ahead) for c in own]
    rear = [lax.ppermute(c, AXIS, back) for c in own]
    mine[1] = front + rear
    for s in range(2, half):
        front = [lax.ppermute(c, AXIS, ahead) for c in front]
        rear = [lax.ppermute(c, AXIS, back) for c in rear]
        if s == 2:
            front[0], rear[0], shipped, small = lax.optimization_barrier(
                (front[0], rear[0], shipped, small)
            )
        mine[s] = front + rear
    at_shift = lax.dynamic_index_in_dim(jnp.asarray(neighbours), me, 0, keepdims=False)
    picked = at_shift[:, None] == jnp.arange(devices)[None, :]
    shift_gates = jnp.sum(jnp.where(picked[:, :, None], small[None, :, :row_count], 0), axis=1)
    shift_gates = shift_gates.astype(jnp.float32) / gate_unit
    slot_codes = small[:, row_count:].reshape(-1)
    slot_length = slot_codes % (block_rows + 1)
    slot_request = slot_codes // (block_rows + 1)


    mine[half] = [lax.ppermute(front[0], AXIS, ahead), lax.ppermute(rear[1], AXIS, back)]
    mine, shipped, shift_gates = lax.optimization_barrier((mine, shipped, shift_gates))
    block_latents = lax.all_to_all(shipped, AXIS, split_axis=0, concat_axis=0, tiled=True)

    parts = {}
    for steps in ([half], list(range(half - 1, -1, -1))):
        both = [mine[s] + [lax.ppermute(c, AXIS, across) for c in mine[s]] for s in steps]
        for s, (part, rest) in zip(steps, mlp(both, gate_up, down_proj)):
            parts[s] = (part, lax.ppermute(rest, AXIS, across))

    def contribution(s, k, flow):
        part, from_other = parts[s]
        size = sizes[flow]
        lo = k * split if s == half else flow * split + (k * row_count if s else 0)
        both = part[lo : lo + size].astype(jnp.float32) + from_other[lo : lo + size].astype(
            jnp.float32
        )
        weight = shift_gates[((-s, s)[k] + chips) % chips, flow * split : flow * split + size]
        return (weight[:, None] * both).astype(jnp.bfloat16)

    key = jnp.where(slot_length > 0, slot_request, decode_count)
    index = jnp.arange(slots)
    before = (key[None, :] < key[:, None]) | (
        (key[None, :] == key[:, None]) & (index[None, :] < index[:, None])
    )
    position = jnp.sum(before, axis=1)
    order = jnp.sum(
        jnp.where(position[None, :] == index[:, None], index[None, :], 0), axis=1
    ).astype(jnp.int32)
    start = jnp.sum(key[None, :] < jnp.arange(decode_count + 1)[:, None], axis=1).astype(jnp.int32)
    first_rows = decode_count // 2

    sums = [{"up": contribution(half, 0, 0)}, {"down": contribution(half, 1, 1)}]
    terms = {
        (s, flow): {"up": contribution(s, 1, flow), "down": contribution(s, 0, flow)}
        for s in range(1, half)
        for flow in range(2)
    }
    last = [contribution(0, 0, flow) for flow in range(2)]
    course = {"up": ahead, "down": back}

    def add(a, b):
        return (a.astype(jnp.float32) + b.astype(jnp.float32)).astype(jnp.bfloat16)

    for s in range(half - 1, -1, -1):
        for flow in range(2):
            moved = {
                way: lax.ppermute(value, AXIS, course[way]) for way, value in sums[flow].items()
            }
            if s == half - 1:
                moved, terms, last, block_latents = lax.optimization_barrier(
                    (moved, terms, last, block_latents)
                )
            else:
                moved = lax.optimization_barrier(moved)
            if s == 0:
                sums[flow] = moved
                continue
            added = {
                way: add(moved[way], term) if way in moved else term
                for way, term in terms[(s, flow)].items()
            }
            if s == 1 and flow == 0:
                early = attend(
                    order, start, slot_length, queries, own_latent, block_latents, 0, first_rows
                )
            if s == 1 and flow == 1:
                added, early = lax.optimization_barrier((added, early))
                late = attend(
                    order,
                    start,
                    slot_length,
                    queries,
                    own_latent,
                    block_latents,
                    first_rows,
                    decode_count - first_rows,
                )
                context = jnp.concatenate([early, late], axis=0)
            sums[flow] = lax.optimization_barrier(added)

    def finish(flow):
        total = sums[flow]["up"].astype(jnp.float32) + sums[flow]["down"].astype(jnp.float32)
        return (total + last[flow].astype(jnp.float32)).astype(jnp.bfloat16)

    return (finish(0), finish(1), context)


def solution(mesh):
    rows = P(("groups", "expert"), None)
    blocks = P(("groups", "expert"), None, None)
    line = P(("groups", "expert"))
    weights = P("expert", None, None)
    return jax.shard_map(
        per_device,
        mesh=mesh,
        in_specs=(rows,) * 6 + (weights, weights, blocks, rows, blocks, line, line, line),
        out_specs=(rows, rows, blocks),
        check_vma=False,
    )
```

```python
import functools

import jax
import jax.numpy as jnp
import numpy as np
from jax import lax
from jax.experimental import pallas as pl
from jax.experimental.pallas import tpu as pltpu
from jax.sharding import PartitionSpec as P

KV = 512
CAPC = 2

softmax_scale = 192.0 ** (-0.5)
gate_unit = 65536.0
AXIS = "expert"
VMEM_LIMIT = 16 << 20


def mlp_kernel(blocks, tile, *refs):
    count = sum(len(sizes) for sizes in blocks)
    total = len(blocks)
    x_refs = refs[:count]
    up_hbm, down_hbm = refs[count : count + 2]
    out_refs = refs[count + 2 : count + 2 + 2 * total]
    rows_ref, up_ref, down_ref, part_ref, hidden_ref = refs[
        count + 2 + 2 * total : count + 7 + 2 * total
    ]
    x_sems, up_sems, down_sems, out_sems = refs[count + 7 + 2 * total :]
    width = up_hbm.shape[0]
    half = down_hbm.shape[0]
    tiles = width // tile
    piece = 256 if half % 256 == 0 else half
    x_copies = []
    at = 0
    for b, sizes in enumerate(blocks):
        copies = []
        row = 0
        for size in sizes:
            copies.append(
                pltpu.make_async_copy(
                    x_refs[at], rows_ref.at[b % 2, pl.ds(row, size)], x_sems.at[at]
                )
            )
            row += size
            at += 1
        x_copies.append(copies)
    def up_copy(k):
        span = pl.ds(pl.multiple_of(k * tile, tile), tile)
        return pltpu.make_async_copy(up_hbm.at[span], up_ref.at[span], up_sems.at[k])

    def down_copy(k):
        span = pl.ds(pl.multiple_of(k * tile, tile), tile)
        return pltpu.make_async_copy(down_hbm.at[:, span], down_ref.at[:, span], down_sems.at[k])

    for copy in x_copies[0]:
        copy.start()
    for k in range(tiles):
        up_copy(k).start()
    for k in range(tiles):
        down_copy(k).start()
    out_copies = []
    for b, sizes in enumerate(blocks):
        slot = b % 2
        rows = sum(sizes)
        if b + 1 < total:
            for copy in x_copies[b + 1]:
                copy.start()
        for copy in x_copies[b]:
            copy.wait()
        if b == 0:
            merged = None
            for k in range(tiles):
                up_copy(k).wait()
                span = slice(k * tile, (k + 1) * tile)
                part = jnp.dot(
                    rows_ref[0, :rows, span], up_ref[span, :], preferred_element_type=jnp.float32
                )
                merged = part if merged is None else merged + part
            value = jax.nn.silu(merged[:, :half]) * merged[:, half:]
            hidden_ref[:rows] = value.astype(jnp.bfloat16)
        else:

            def up_step(j, _, slot=slot, rows=rows):
                at = pl.multiple_of(j * piece, piece)
                here = rows_ref[slot, :rows]
                gate = jnp.dot(
                    here, up_ref[:, pl.ds(at, piece)], preferred_element_type=jnp.float32
                )
                up = jnp.dot(
                    here, up_ref[:, pl.ds(half + at, piece)], preferred_element_type=jnp.float32
                )
                value = jax.nn.silu(gate) * up
                hidden_ref[:rows, pl.ds(at, piece)] = value.astype(jnp.bfloat16)
                return 0

            lax.fori_loop(0, half // piece, up_step, 0)
        if b >= 2:
            for copy in out_copies[b - 2]:
                copy.wait()

        def down_step(k, _, b=b, slot=slot, rows=rows):
            if b == 0:
                down_copy(k).wait()
            span = pl.ds(pl.multiple_of(k * tile, tile), tile)
            part = jnp.dot(
                hidden_ref[:rows], down_ref[:, span], preferred_element_type=jnp.float32
            )
            part_ref[slot, :rows, span] = part.astype(jnp.bfloat16)
            return 0

        lax.fori_loop(0, tiles, down_step, 0)
        size = rows // 2
        copies = []
        for c in range(2):
            copy = pltpu.make_async_copy(
                part_ref.at[slot, pl.ds(c * size, size)], out_refs[2 * b + c], out_sems.at[b, c]
            )
            copy.start()
            copies.append(copy)
        out_copies.append(copies)
    for copies in out_copies[-2:]:
        for copy in copies:
            copy.wait()


def mlp(blocks, gate_up, down_proj):
    width, both = gate_up.shape
    half = down_proj.shape[0]
    tile = width // 4 if width % 512 == 0 else width
    tiles = width // tile
    sizes = tuple(tuple(c.shape[0] for c in chunks) for chunks in blocks)
    counts = [sum(block) for block in sizes]
    chunks = [c for block in blocks for c in block]
    rows = sum(counts)
    anywhere = pl.BlockSpec(memory_space=pl.ANY)
    dma = pltpu.SemaphoreType.DMA
    results = pl.pallas_call(
        functools.partial(mlp_kernel, sizes, tile),
        in_specs=[anywhere] * len(chunks) + [pl.BlockSpec(memory_space=pltpu.HBM)] * 2,
        out_specs=[anywhere] * (2 * len(blocks)),
        out_shape=[
            jax.ShapeDtypeStruct((n // 2, width), jnp.bfloat16) for n in counts for _ in range(2)
        ],
        scratch_shapes=[
            pltpu.VMEM((2, max(counts), width), jnp.bfloat16),
            pltpu.VMEM((width, both), jnp.bfloat16),
            pltpu.VMEM((half, width), jnp.bfloat16),
            pltpu.VMEM((2, max(counts), width), jnp.bfloat16),
            pltpu.VMEM((max(counts), half), jnp.bfloat16),
            dma((len(chunks),)),
            dma((tiles,)),
            dma((tiles,)),
            dma((len(blocks), 2)),
        ],
        compiler_params=pltpu.CompilerParams(vmem_limit_bytes=46 << 20),
        cost_estimate=pl.CostEstimate(
            flops=6 * rows * width * half,
            bytes_accessed=6 * width * half + 4 * rows * width,
            transcendentals=rows * half,
        ),
        name="mlp",
    )(*chunks, gate_up, down_proj)
    return [(results[2 * b], results[2 * b + 1]) for b in range(len(blocks))]


def ship_kernel(source_ref, block_ref, out_ref):
    for i in range(out_ref.shape[0]):
        out_ref[i] = block_ref[source_ref[i]]


def ship_blocks(latents, source):
    slots = source.shape[0]
    resident = pl.BlockSpec(memory_space=pltpu.VMEM)
    return pl.pallas_call(
        ship_kernel,
        in_specs=[pl.BlockSpec(memory_space=pltpu.SMEM), resident],
        out_specs=resident,
        out_shape=jax.ShapeDtypeStruct((slots,) + latents.shape[1:], latents.dtype),
        compiler_params=pltpu.CompilerParams(vmem_limit_bytes=16 << 20),
        cost_estimate=pl.CostEstimate(
            flops=0, bytes_accessed=6 * latents.size, transcendentals=0
        ),
        name="ship",
    )(source, latents)


def attend_kernel(order_ref, start_ref, length_ref, query_ref, own_ref, latent_ref, out_ref):
    row = pl.program_id(0)
    query = query_ref[0]
    own = own_ref[0].astype(jnp.float32)
    own_score = (
        jnp.sum(query.astype(jnp.float32) * own, axis=1, keepdims=True) * softmax_scale
    )
    heads = query.shape[0]
    block = latent_ref.shape[1]

    def step(j, state):
        top, total, value = state
        slot = order_ref[j]
        latent = latent_ref[slot]
        scores = (
            lax.dot_general(
                query, latent, (((1,), (1,)), ((), ())), preferred_element_type=jnp.float32
            )
            * softmax_scale
        )
        inside = lax.broadcasted_iota(jnp.int32, (heads, block), 1) < length_ref[slot]
        span_max = jnp.max(jnp.where(inside, scores, -jnp.inf), axis=1, keepdims=True)
        weights = jnp.where(inside, jnp.exp(scores - span_max), 0.0)
        span_total = jnp.sum(weights, axis=1, keepdims=True)
        span_value = jnp.dot(
            weights.astype(jnp.bfloat16), latent[:, :KV], preferred_element_type=jnp.float32
        )
        higher = jnp.maximum(top, span_max)
        old = jnp.exp(top - higher)
        new = jnp.exp(span_max - higher)
        return (higher, old * total + new * span_total, old * value + new * span_value)

    state = (
        own_score,
        jnp.ones((heads, 1), jnp.float32),
        jnp.broadcast_to(own[:, :KV], (heads, KV)),
    )
    top, total, value = lax.fori_loop(start_ref[row], start_ref[row + 1], step, state)
    out_ref[0] = (value / total).astype(jnp.bfloat16)


def attend(order, start, lengths, queries, own_latent, latents, first, rows):
    _, heads, width = queries.shape
    slots, block, _ = latents.shape
    own_latent = own_latent.reshape(own_latent.shape[0], 1, width)
    return pl.pallas_call(
        attend_kernel,
        grid_spec=pltpu.PrefetchScalarGridSpec(
            num_scalar_prefetch=3,
            grid=(rows,),
            in_specs=[
                pl.BlockSpec((1, heads, width), lambda i, *_: (i + first, 0, 0)),
                pl.BlockSpec((1, 1, width), lambda i, *_: (i + first, 0, 0)),
                pl.BlockSpec((slots, block, width), lambda i, *_: (0, 0, 0)),
            ],
            out_specs=pl.BlockSpec((1, heads, KV), lambda i, *_: (i, 0, 0)),
        ),
        out_shape=jax.ShapeDtypeStruct((rows, heads, KV), jnp.bfloat16),
        compiler_params=pltpu.CompilerParams(vmem_limit_bytes=VMEM_LIMIT),
        cost_estimate=pl.CostEstimate(
            flops=2 * slots * heads * block * width,
            bytes_accessed=2 * (rows * heads * (width + KV) + slots * block * width),
            transcendentals=slots * heads * block,
        ),
        name="attend",
    )(order, start[first : first + rows + 1], lengths, queries, own_latent, latents)


def dense_gates(experts, gates, expert_count):
    named = experts[:, :, None] == jnp.arange(expert_count)[None, None, :]
    return jnp.sum(jnp.where(named, gates[:, :, None], 0), axis=1)


def per_device(
    prefill_tokens,
    prefill_experts,
    prefill_gates,
    decode_rows,
    decode_experts,
    decode_gates,
    w_gate_up,
    w_down,
    queries,
    own_latent,
    latents,
    span_owner,
    span_request,
    span_length,
):
    devices = lax.axis_size(AXIS)
    chips = devices // 2
    half = chips // 2
    gate_up = w_gate_up[0]
    down_proj = w_down[0]
    prefill_count = prefill_tokens.shape[0]
    decode_count = decode_rows.shape[0]
    row_count = prefill_count + decode_count
    split = prefill_count

    ring = list(range(0, chips, 2)) + list(range(1, chips, 2))[::-1]
    place_of = np.zeros(chips, np.int32)
    for i, chip in enumerate(ring):
        place_of[chip] = i
    ahead = [
        (2 * ring[i] + c, 2 * ring[(i + 1) % chips] + c) for i in range(chips) for c in range(2)
    ]
    back = [(b, a) for a, b in ahead]
    across = [(i, i ^ 1) for i in range(devices)]
    me = lax.axis_index(AXIS)
    neighbours = np.zeros((devices, chips), np.int32)
    for device in range(devices):
        for shift in range(chips):
            chip = ring[(place_of[device // 2] + shift) % chips]
            neighbours[device, shift] = 2 * chip + device % 2

    span_count = span_owner.shape[0]
    block_rows = latents.shape[1]
    slots = devices * CAPC
    numbered = jnp.arange(span_count)
    earlier = (span_owner[None, :] == span_owner[:, None]) & (numbered[None, :] < numbered[:, None])
    span_rank = jnp.sum(earlier, axis=1)
    slot_of = span_owner * CAPC + span_rank
    placed = slot_of[None, :] == jnp.arange(slots)[:, None]
    source = jnp.sum(jnp.where(placed, numbered[None, :], 0), axis=1).astype(jnp.int32)
    codes = span_request * (block_rows + 1) + span_length
    slot_codes = jnp.sum(jnp.where(placed, codes[None, :], 0), axis=1).astype(jnp.int32)

    gates = jnp.concatenate(
        [
            dense_gates(prefill_experts, prefill_gates, chips),
            dense_gates(decode_experts, decode_gates, chips),
        ],
        axis=0,
    )
    small = jnp.concatenate(
        [jnp.repeat(gates.T, 2, axis=0), slot_codes.reshape(devices, CAPC)], axis=1
    ).astype(jnp.int32)
    small = lax.all_to_all(small, AXIS, split_axis=0, concat_axis=0, tiled=True)
    shipped = ship_blocks(latents, source)

    own = [prefill_tokens, decode_rows]
    sizes = [prefill_count, decode_count]
    mine = {0: own}
    front = [lax.ppermute(c, AXIS, ahead) for c in own]
    rear = [lax.ppermute(c, AXIS, back) for c in own]
    front[0], rear[0], shipped, small = lax.optimization_barrier(
        (front[0], rear[0], shipped, small)
    )
    mine[1] = front + rear
    for s in range(2, half):
        front = [lax.ppermute(c, AXIS, ahead) for c in front]
        rear = [lax.ppermute(c, AXIS, back) for c in rear]
        mine[s] = front + rear
    at_shift = lax.dynamic_index_in_dim(jnp.asarray(neighbours), me, 0, keepdims=False)
    picked = at_shift[:, None] == jnp.arange(devices)[None, :]
    shift_gates = jnp.sum(jnp.where(picked[:, :, None], small[None, :, :row_count], 0), axis=1)
    shift_gates = shift_gates.astype(jnp.float32) / gate_unit
    slot_codes = small[:, row_count:].reshape(-1)
    slot_length = slot_codes % (block_rows + 1)
    slot_request = slot_codes // (block_rows + 1)


    mine[half] = [lax.ppermute(front[0], AXIS, ahead), lax.ppermute(rear[1], AXIS, back)]
    mine, shipped, shift_gates = lax.optimization_barrier((mine, shipped, shift_gates))
    block_latents = lax.all_to_all(shipped, AXIS, split_axis=0, concat_axis=0, tiled=True)

    parts = {}
    groups = [[half], [half - 1], list(range(half - 2, -1, -1))]
    for group in groups:
        both = [mine[s] + [lax.ppermute(c, AXIS, across) for c in mine[s]] for s in group]
        for s, (part, rest) in zip(group, mlp(both, gate_up, down_proj)):
            parts[s] = (part, lax.ppermute(rest, AXIS, across))

    def contribution(s, k, flow):
        part, from_other = parts[s]
        size = sizes[flow]
        lo = k * split if s == half else flow * split + (k * row_count if s else 0)
        both = part[lo : lo + size].astype(jnp.float32) + from_other[lo : lo + size].astype(
            jnp.float32
        )
        weight = shift_gates[((-s, s)[k] + chips) % chips, flow * split : flow * split + size]
        return (weight[:, None] * both).astype(jnp.bfloat16)

    key = jnp.where(slot_length > 0, slot_request, decode_count)
    index = jnp.arange(slots)
    before = (key[None, :] < key[:, None]) | (
        (key[None, :] == key[:, None]) & (index[None, :] < index[:, None])
    )
    position = jnp.sum(before, axis=1)
    order = jnp.sum(
        jnp.where(position[None, :] == index[:, None], index[None, :], 0), axis=1
    ).astype(jnp.int32)
    start = jnp.sum(key[None, :] < jnp.arange(decode_count + 1)[:, None], axis=1).astype(jnp.int32)
    first_rows = decode_count // 2

    sums = [{"up": contribution(half, 0, 0)}, {"down": contribution(half, 1, 1)}]
    terms = {
        (s, flow): {"up": contribution(s, 1, flow), "down": contribution(s, 0, flow)}
        for s in range(1, half)
        for flow in range(2)
    }
    last = [contribution(0, 0, flow) for flow in range(2)]
    course = {"up": ahead, "down": back}

    def add(a, b):
        return (a.astype(jnp.float32) + b.astype(jnp.float32)).astype(jnp.bfloat16)

    for s in range(half - 1, -1, -1):
        for flow in range(2):
            moved = {
                way: lax.ppermute(value, AXIS, course[way]) for way, value in sums[flow].items()
            }
            if s == half - 1:
                moved, terms, last, block_latents = lax.optimization_barrier(
                    (moved, terms, last, block_latents)
                )
            else:
                moved = lax.optimization_barrier(moved)
            if s == 0:
                sums[flow] = moved
                continue
            added = {
                way: add(moved[way], term) if way in moved else term
                for way, term in terms[(s, flow)].items()
            }
            if s == 1 and flow == 0:
                early = attend(
                    order, start, slot_length, queries, own_latent, block_latents, 0, first_rows
                )
            if s == 1 and flow == 1:
                added, early = lax.optimization_barrier((added, early))
                late = attend(
                    order,
                    start,
                    slot_length,
                    queries,
                    own_latent,
                    block_latents,
                    first_rows,
                    decode_count - first_rows,
                )
                context = jnp.concatenate([early, late], axis=0)
            sums[flow] = lax.optimization_barrier(added)

    def finish(flow):
        total = sums[flow]["up"].astype(jnp.float32) + sums[flow]["down"].astype(jnp.float32)
        return (total + last[flow].astype(jnp.float32)).astype(jnp.bfloat16)

    return (finish(0), finish(1), context)


def solution(mesh):
    rows = P(("groups", "expert"), None)
    blocks = P(("groups", "expert"), None, None)
    line = P(("groups", "expert"))
    weights = P("expert", None, None)
    return jax.shard_map(
        per_device,
        mesh=mesh,
        in_specs=(rows,) * 6 + (weights, weights, blocks, rows, blocks, line, line, line),
        out_specs=(rows, rows, blocks),
        check_vma=False,
    )
```

```python
import functools

import jax
import jax.numpy as jnp
import numpy as np
from jax import lax
from jax.experimental import pallas as pl
from jax.experimental.pallas import tpu as pltpu
from jax.sharding import PartitionSpec as P

KV = 512
CAPC = 2

softmax_scale = 192.0 ** (-0.5)
gate_unit = 65536.0
AXIS = "expert"
VMEM_LIMIT = 16 << 20


def mlp_kernel(sizes, tile, *refs):
    count = len(sizes)
    x_refs = refs[:count]
    up_hbm, down_hbm, mine_hbm, other_hbm = refs[count : count + 4]
    rows_ref, up_ref, down_ref, part_ref, x_sems, up_sems, down_sems, out_sems = refs[count + 4 :]
    width = up_hbm.shape[0]
    half = down_hbm.shape[0]
    tiles = width // tile
    size = mine_hbm.shape[0]
    spans = [pl.ds(k * tile, tile) for k in range(tiles)]
    starts = [sum(sizes[:c]) for c in range(count)]
    x_copies = [
        [
            pltpu.make_async_copy(
                x_refs[c].at[:, spans[k]],
                rows_ref.at[pl.ds(starts[c], sizes[c]), spans[k]],
                x_sems.at[c, k],
            )
            for c in range(count)
        ]
        for k in range(tiles)
    ]
    up_copies = [
        pltpu.make_async_copy(up_hbm.at[s], up_ref.at[s], up_sems.at[k])
        for k, s in enumerate(spans)
    ]
    down_copies = [
        pltpu.make_async_copy(down_hbm.at[:, s], down_ref.at[:, s], down_sems.at[k])
        for k, s in enumerate(spans)
    ]
    for k in range(tiles):
        for copy in x_copies[k]:
            copy.start()
        up_copies[k].start()
    for copy in down_copies:
        copy.start()
    merged = None
    for k in range(tiles):
        for copy in x_copies[k]:
            copy.wait()
        up_copies[k].wait()
        cols = slice(k * tile, (k + 1) * tile)
        part = jnp.dot(rows_ref[:, cols], up_ref[cols, :], preferred_element_type=jnp.float32)
        merged = part if merged is None else merged + part
    hidden = (jax.nn.silu(merged[:, :half]) * merged[:, half:]).astype(jnp.bfloat16)
    out_copies = []
    for n, s in enumerate(spans):
        down_copies[n].wait()
        cols = slice(n * tile, (n + 1) * tile)
        part = jnp.dot(hidden, down_ref[:, cols], preferred_element_type=jnp.float32)
        part_ref[:, cols] = part.astype(jnp.bfloat16)
        for c, target in enumerate((mine_hbm, other_hbm)):
            copy = pltpu.make_async_copy(
                part_ref.at[pl.ds(c * size, size), s], target.at[:, s], out_sems.at[c, n]
            )
            copy.start()
            out_copies.append(copy)
    for copy in out_copies:
        copy.wait()


def mlp(mine, other, gate_up, down_proj, tile=1024):
    chunks = mine + other
    width, both = gate_up.shape
    half = down_proj.shape[0]
    tile = tile if width % tile == 0 else width
    tiles = width // tile
    sizes = tuple(c.shape[0] for c in chunks)
    rows = sum(sizes)
    anywhere = pl.BlockSpec(memory_space=pl.ANY)
    dma = pltpu.SemaphoreType.DMA
    return pl.pallas_call(
        functools.partial(mlp_kernel, sizes, tile),
        in_specs=[anywhere] * len(chunks) + [pl.BlockSpec(memory_space=pltpu.HBM)] * 2,
        out_specs=[anywhere, anywhere],
        out_shape=[jax.ShapeDtypeStruct((rows // 2, width), jnp.bfloat16)] * 2,
        scratch_shapes=[
            pltpu.VMEM((rows, width), jnp.bfloat16),
            pltpu.VMEM((width, both), jnp.bfloat16),
            pltpu.VMEM((half, width), jnp.bfloat16),
            pltpu.VMEM((rows, width), jnp.bfloat16),
            dma((len(chunks), tiles)),
            dma((tiles,)),
            dma((tiles,)),
            dma((2, tiles)),
        ],
        compiler_params=pltpu.CompilerParams(vmem_limit_bytes=44 << 20),
        cost_estimate=pl.CostEstimate(
            flops=6 * rows * width * half,
            bytes_accessed=6 * width * half + 4 * rows * width,
            transcendentals=rows * half,
        ),
        name="mlp",
    )(*chunks, gate_up, down_proj)


def ship_kernel(source_ref, block_ref, out_ref):
    for i in range(out_ref.shape[0]):
        out_ref[i] = block_ref[source_ref[i]]


def ship_blocks(latents, source):
    slots = source.shape[0]
    resident = pl.BlockSpec(memory_space=pltpu.VMEM)
    return pl.pallas_call(
        ship_kernel,
        in_specs=[pl.BlockSpec(memory_space=pltpu.SMEM), resident],
        out_specs=resident,
        out_shape=jax.ShapeDtypeStruct((slots,) + latents.shape[1:], latents.dtype),
        compiler_params=pltpu.CompilerParams(vmem_limit_bytes=16 << 20),
        cost_estimate=pl.CostEstimate(
            flops=0, bytes_accessed=6 * latents.size, transcendentals=0
        ),
        name="ship",
    )(source, latents)


def attend_kernel(order_ref, start_ref, length_ref, query_ref, own_ref, latent_ref, out_ref):
    row = pl.program_id(0)
    query = query_ref[0]
    own = own_ref[0].astype(jnp.float32)
    own_score = (
        jnp.sum(query.astype(jnp.float32) * own, axis=1, keepdims=True) * softmax_scale
    )
    heads = query.shape[0]
    block = latent_ref.shape[1]

    def step(j, state):
        top, total, value = state
        slot = order_ref[j]
        latent = latent_ref[slot]
        scores = (
            lax.dot_general(
                query, latent, (((1,), (1,)), ((), ())), preferred_element_type=jnp.float32
            )
            * softmax_scale
        )
        inside = lax.broadcasted_iota(jnp.int32, (heads, block), 1) < length_ref[slot]
        span_max = jnp.max(jnp.where(inside, scores, -jnp.inf), axis=1, keepdims=True)
        weights = jnp.where(inside, jnp.exp(scores - span_max), 0.0)
        span_total = jnp.sum(weights, axis=1, keepdims=True)
        span_value = jnp.dot(
            weights.astype(jnp.bfloat16), latent[:, :KV], preferred_element_type=jnp.float32
        )
        higher = jnp.maximum(top, span_max)
        old = jnp.exp(top - higher)
        new = jnp.exp(span_max - higher)
        return (higher, old * total + new * span_total, old * value + new * span_value)

    state = (
        own_score,
        jnp.ones((heads, 1), jnp.float32),
        jnp.broadcast_to(own[:, :KV], (heads, KV)),
    )
    top, total, value = lax.fori_loop(start_ref[row], start_ref[row + 1], step, state)
    out_ref[0] = (value / total).astype(jnp.bfloat16)


def attend(order, start, lengths, queries, own_latent, latents, first, rows):
    _, heads, width = queries.shape
    slots, block, _ = latents.shape
    own_latent = own_latent.reshape(own_latent.shape[0], 1, width)
    return pl.pallas_call(
        attend_kernel,
        grid_spec=pltpu.PrefetchScalarGridSpec(
            num_scalar_prefetch=3,
            grid=(rows,),
            in_specs=[
                pl.BlockSpec((1, heads, width), lambda i, *_: (i + first, 0, 0)),
                pl.BlockSpec((1, 1, width), lambda i, *_: (i + first, 0, 0)),
                pl.BlockSpec((slots, block, width), lambda i, *_: (0, 0, 0)),
            ],
            out_specs=pl.BlockSpec((1, heads, KV), lambda i, *_: (i, 0, 0)),
        ),
        out_shape=jax.ShapeDtypeStruct((rows, heads, KV), jnp.bfloat16),
        compiler_params=pltpu.CompilerParams(vmem_limit_bytes=VMEM_LIMIT),
        cost_estimate=pl.CostEstimate(
            flops=2 * slots * heads * block * width,
            bytes_accessed=2 * (rows * heads * (width + KV) + slots * block * width),
            transcendentals=slots * heads * block,
        ),
        name="attend",
    )(order, start[first : first + rows + 1], lengths, queries, own_latent, latents)


def dense_gates(experts, gates, expert_count):
    named = experts[:, :, None] == jnp.arange(expert_count)[None, None, :]
    return jnp.sum(jnp.where(named, gates[:, :, None], 0), axis=1)


def per_device(
    prefill_tokens,
    prefill_experts,
    prefill_gates,
    decode_rows,
    decode_experts,
    decode_gates,
    w_gate_up,
    w_down,
    queries,
    own_latent,
    latents,
    span_owner,
    span_request,
    span_length,
):
    devices = lax.axis_size(AXIS)
    chips = devices // 2
    half = chips // 2
    gate_up = w_gate_up[0]
    down_proj = w_down[0]
    prefill_count = prefill_tokens.shape[0]
    decode_count = decode_rows.shape[0]
    row_count = prefill_count + decode_count
    split = prefill_count

    ring = list(range(0, chips, 2)) + list(range(1, chips, 2))[::-1]
    place_of = np.zeros(chips, np.int32)
    for i, chip in enumerate(ring):
        place_of[chip] = i
    ahead = [
        (2 * ring[i] + c, 2 * ring[(i + 1) % chips] + c) for i in range(chips) for c in range(2)
    ]
    back = [(b, a) for a, b in ahead]
    across = [(i, i ^ 1) for i in range(devices)]
    me = lax.axis_index(AXIS)
    neighbours = np.zeros((devices, chips), np.int32)
    for device in range(devices):
        for shift in range(chips):
            chip = ring[(place_of[device // 2] + shift) % chips]
            neighbours[device, shift] = 2 * chip + device % 2

    span_count = span_owner.shape[0]
    block_rows = latents.shape[1]
    slots = devices * CAPC
    numbered = jnp.arange(span_count)
    earlier = (span_owner[None, :] == span_owner[:, None]) & (numbered[None, :] < numbered[:, None])
    span_rank = jnp.sum(earlier, axis=1)
    slot_of = span_owner * CAPC + span_rank
    placed = slot_of[None, :] == jnp.arange(slots)[:, None]
    source = jnp.sum(jnp.where(placed, numbered[None, :], 0), axis=1).astype(jnp.int32)
    codes = span_request * (block_rows + 1) + span_length
    slot_codes = jnp.sum(jnp.where(placed, codes[None, :], 0), axis=1).astype(jnp.int32)

    gates = jnp.concatenate(
        [
            dense_gates(prefill_experts, prefill_gates, chips),
            dense_gates(decode_experts, decode_gates, chips),
        ],
        axis=0,
    )
    small = jnp.concatenate(
        [jnp.repeat(gates.T, 2, axis=0), slot_codes.reshape(devices, CAPC)], axis=1
    ).astype(jnp.int32)
    small = lax.all_to_all(small, AXIS, split_axis=0, concat_axis=0, tiled=True)
    shipped = ship_blocks(latents, source)

    own = [prefill_tokens, decode_rows]
    sizes = [prefill_count, decode_count]
    front = {1: [lax.ppermute(c, AXIS, ahead) for c in own]}
    rear = {1: [lax.ppermute(c, AXIS, back) for c in own]}
    front[1][0], rear[1][0], shipped, small = lax.optimization_barrier(
        (front[1][0], rear[1][0], shipped, small)
    )
    at_shift = lax.dynamic_index_in_dim(jnp.asarray(neighbours), me, 0, keepdims=False)
    picked = at_shift[:, None] == jnp.arange(devices)[None, :]
    shift_gates = jnp.sum(jnp.where(picked[:, :, None], small[None, :, :row_count], 0), axis=1)
    shift_gates = shift_gates.astype(jnp.float32) / gate_unit
    slot_codes = small[:, row_count:].reshape(-1)
    slot_length = slot_codes % (block_rows + 1)
    slot_request = slot_codes // (block_rows + 1)

    for s in range(2, half):
        front[s] = [lax.ppermute(c, AXIS, ahead) for c in front[s - 1]]
        rear[s] = [lax.ppermute(c, AXIS, back) for c in rear[s - 1]]

    def work(s, mine):
        other = [lax.ppermute(c, AXIS, across) for c in mine]
        return mlp(mine, other, gate_up, down_proj)

    first = min(2, half - 1)
    near, _ = lax.optimization_barrier((front[1] + rear[1] + own, front[first][1:]))
    results = {1: work(1, near)}
    last_rear, results[1] = lax.optimization_barrier((rear[half - 1][1], results[1]))
    front[half] = [lax.ppermute(front[half - 1][0], AXIS, ahead)]
    rear[half] = [lax.ppermute(last_rear, AXIS, back)]
    front, rear, shipped, shift_gates = lax.optimization_barrier(
        (front, rear, shipped, shift_gates)
    )
    block_latents = lax.all_to_all(shipped, AXIS, split_axis=0, concat_axis=0, tiled=True)
    for s in range(half, 1, -1):
        results[s] = work(s, front[s] + rear[s])
    parts = {s: (part, lax.ppermute(rest, AXIS, across)) for s, (part, rest) in results.items()}

    def contribution(s, k, flow):
        part, from_other = parts[max(s, 1)]
        size = sizes[flow]
        lo = flow * split
        if s == half:
            lo = k * split
        elif s == 0:
            lo = lo + 2 * row_count
        else:
            lo = lo + k * row_count
        both = part[lo : lo + size].astype(jnp.float32) + from_other[lo : lo + size].astype(
            jnp.float32
        )
        weight = shift_gates[((-s, s)[k] + chips) % chips, flow * split : flow * split + size]
        return (weight[:, None] * both).astype(jnp.bfloat16)

    key = jnp.where(slot_length > 0, slot_request, decode_count)
    index = jnp.arange(slots)
    before = (key[None, :] < key[:, None]) | (
        (key[None, :] == key[:, None]) & (index[None, :] < index[:, None])
    )
    position = jnp.sum(before, axis=1)
    order = jnp.sum(
        jnp.where(position[None, :] == index[:, None], index[None, :], 0), axis=1
    ).astype(jnp.int32)
    start = jnp.sum(key[None, :] < jnp.arange(decode_count + 1)[:, None], axis=1).astype(jnp.int32)
    first_rows = decode_count // 2

    sums = [{"up": contribution(half, 0, 0)}, {"down": contribution(half, 1, 1)}]
    terms = {
        (s, flow): {"up": contribution(s, 1, flow), "down": contribution(s, 0, flow)}
        for s in range(1, half)
        for flow in range(2)
    }
    last = [contribution(0, 0, flow) for flow in range(2)]
    course = {"up": ahead, "down": back}

    def add(a, b):
        return (a.astype(jnp.float32) + b.astype(jnp.float32)).astype(jnp.bfloat16)

    for s in range(half - 1, -1, -1):
        for flow in range(2):
            moved = {
                way: lax.ppermute(value, AXIS, course[way]) for way, value in sums[flow].items()
            }
            if s == half - 1:
                moved, terms, last, block_latents = lax.optimization_barrier(
                    (moved, terms, last, block_latents)
                )
            else:
                moved = lax.optimization_barrier(moved)
            if s == 0:
                sums[flow] = moved
                continue
            added = {
                way: add(moved[way], term) if way in moved else term
                for way, term in terms[(s, flow)].items()
            }
            if s == 1 and flow == 0:
                early = attend(
                    order, start, slot_length, queries, own_latent, block_latents, 0, first_rows
                )
            if s == 1 and flow == 1:
                added, early = lax.optimization_barrier((added, early))
                late = attend(
                    order,
                    start,
                    slot_length,
                    queries,
                    own_latent,
                    block_latents,
                    first_rows,
                    decode_count - first_rows,
                )
                context = jnp.concatenate([early, late], axis=0)
            sums[flow] = lax.optimization_barrier(added)

    def finish(flow):
        total = sums[flow]["up"].astype(jnp.float32) + sums[flow]["down"].astype(jnp.float32)
        return (total + last[flow].astype(jnp.float32)).astype(jnp.bfloat16)

    return (finish(0), finish(1), context)


def solution(mesh):
    rows = P(("groups", "expert"), None)
    blocks = P(("groups", "expert"), None, None)
    line = P(("groups", "expert"))
    weights = P("expert", None, None)
    return jax.shard_map(
        per_device,
        mesh=mesh,
        in_specs=(rows,) * 6 + (weights, weights, blocks, rows, blocks, line, line, line),
        out_specs=(rows, rows, blocks),
        check_vma=False,
    )
```

```python
import functools

import jax
import jax.numpy as jnp
import numpy as np
from jax import lax
from jax.experimental import pallas as pl
from jax.experimental.pallas import tpu as pltpu
from jax.sharding import PartitionSpec as P

KV = 512
CAPC = 2

softmax_scale = 192.0 ** (-0.5)
gate_unit = 65536.0
AXIS = "expert"
VMEM_LIMIT = 16 << 20


def mlp_kernel(sizes, tile, *refs):
    count = len(sizes)
    x_refs = refs[:count]
    up_hbm, down_hbm, mine_hbm, other_hbm = refs[count : count + 4]
    rows_ref, up_ref, down_ref, part_ref, x_sems, up_sems, down_sems, out_sems = refs[count + 4 :]
    width = up_hbm.shape[0]
    half = down_hbm.shape[0]
    tiles = width // tile
    size = mine_hbm.shape[0]
    spans = [pl.ds(k * tile, tile) for k in range(tiles)]
    starts = [sum(sizes[:c]) for c in range(count)]
    x_copies = [
        [
            pltpu.make_async_copy(
                x_refs[c].at[:, spans[k]],
                rows_ref.at[pl.ds(starts[c], sizes[c]), spans[k]],
                x_sems.at[c, k],
            )
            for c in range(count)
        ]
        for k in range(tiles)
    ]
    up_copies = [
        pltpu.make_async_copy(up_hbm.at[s], up_ref.at[s], up_sems.at[k])
        for k, s in enumerate(spans)
    ]
    down_copies = [
        pltpu.make_async_copy(down_hbm.at[:, s], down_ref.at[:, s], down_sems.at[k])
        for k, s in enumerate(spans)
    ]
    for k in range(tiles):
        for copy in x_copies[k]:
            copy.start()
        up_copies[k].start()
    for copy in down_copies:
        copy.start()
    merged = None
    for k in range(tiles):
        for copy in x_copies[k]:
            copy.wait()
        up_copies[k].wait()
        cols = slice(k * tile, (k + 1) * tile)
        part = jnp.dot(rows_ref[:, cols], up_ref[cols, :], preferred_element_type=jnp.float32)
        merged = part if merged is None else merged + part
    hidden = (jax.nn.silu(merged[:, :half]) * merged[:, half:]).astype(jnp.bfloat16)
    out_copies = []
    for n, s in enumerate(spans):
        down_copies[n].wait()
        cols = slice(n * tile, (n + 1) * tile)
        part = jnp.dot(hidden, down_ref[:, cols], preferred_element_type=jnp.float32)
        part_ref[:, cols] = part.astype(jnp.bfloat16)
        for c, target in enumerate((mine_hbm, other_hbm)):
            copy = pltpu.make_async_copy(
                part_ref.at[pl.ds(c * size, size), s], target.at[:, s], out_sems.at[c, n]
            )
            copy.start()
            out_copies.append(copy)
    for copy in out_copies:
        copy.wait()


def mlp(mine, other, gate_up, down_proj, tile=1024):
    chunks = mine + other
    width, both = gate_up.shape
    half = down_proj.shape[0]
    tile = tile if width % tile == 0 else width
    tiles = width // tile
    sizes = tuple(c.shape[0] for c in chunks)
    rows = sum(sizes)
    anywhere = pl.BlockSpec(memory_space=pl.ANY)
    dma = pltpu.SemaphoreType.DMA
    return pl.pallas_call(
        functools.partial(mlp_kernel, sizes, tile),
        in_specs=[anywhere] * len(chunks) + [pl.BlockSpec(memory_space=pltpu.HBM)] * 2,
        out_specs=[anywhere, anywhere],
        out_shape=[jax.ShapeDtypeStruct((rows // 2, width), jnp.bfloat16)] * 2,
        scratch_shapes=[
            pltpu.VMEM((rows, width), jnp.bfloat16),
            pltpu.VMEM((width, both), jnp.bfloat16),
            pltpu.VMEM((half, width), jnp.bfloat16),
            pltpu.VMEM((rows, width), jnp.bfloat16),
            dma((len(chunks), tiles)),
            dma((tiles,)),
            dma((tiles,)),
            dma((2, tiles)),
        ],
        compiler_params=pltpu.CompilerParams(vmem_limit_bytes=44 << 20),
        cost_estimate=pl.CostEstimate(
            flops=6 * rows * width * half,
            bytes_accessed=6 * width * half + 4 * rows * width,
            transcendentals=rows * half,
        ),
        name="mlp",
    )(*chunks, gate_up, down_proj)


def ship_kernel(source_ref, block_ref, out_ref):
    for i in range(out_ref.shape[0]):
        out_ref[i] = block_ref[source_ref[i]]


def ship_blocks(latents, source):
    slots = source.shape[0]
    resident = pl.BlockSpec(memory_space=pltpu.VMEM)
    return pl.pallas_call(
        ship_kernel,
        in_specs=[pl.BlockSpec(memory_space=pltpu.SMEM), resident],
        out_specs=resident,
        out_shape=jax.ShapeDtypeStruct((slots,) + latents.shape[1:], latents.dtype),
        compiler_params=pltpu.CompilerParams(vmem_limit_bytes=16 << 20),
        cost_estimate=pl.CostEstimate(
            flops=0, bytes_accessed=6 * latents.size, transcendentals=0
        ),
        name="ship",
    )(source, latents)


def attend_kernel(order_ref, start_ref, length_ref, query_ref, own_ref, latent_ref, out_ref):
    row = pl.program_id(0)
    query = query_ref[0]
    own = own_ref[0].astype(jnp.float32)
    own_score = (
        jnp.sum(query.astype(jnp.float32) * own, axis=1, keepdims=True) * softmax_scale
    )
    heads = query.shape[0]
    block = latent_ref.shape[1]

    def step(j, state):
        top, total, value = state
        slot = order_ref[j]
        latent = latent_ref[slot]
        scores = (
            lax.dot_general(
                query, latent, (((1,), (1,)), ((), ())), preferred_element_type=jnp.float32
            )
            * softmax_scale
        )
        inside = lax.broadcasted_iota(jnp.int32, (heads, block), 1) < length_ref[slot]
        span_max = jnp.max(jnp.where(inside, scores, -jnp.inf), axis=1, keepdims=True)
        weights = jnp.where(inside, jnp.exp(scores - span_max), 0.0)
        span_total = jnp.sum(weights, axis=1, keepdims=True)
        span_value = jnp.dot(
            weights.astype(jnp.bfloat16), latent[:, :KV], preferred_element_type=jnp.float32
        )
        higher = jnp.maximum(top, span_max)
        old = jnp.exp(top - higher)
        new = jnp.exp(span_max - higher)
        return (higher, old * total + new * span_total, old * value + new * span_value)

    state = (
        own_score,
        jnp.ones((heads, 1), jnp.float32),
        jnp.broadcast_to(own[:, :KV], (heads, KV)),
    )
    top, total, value = lax.fori_loop(start_ref[row], start_ref[row + 1], step, state)
    out_ref[0] = (value / total).astype(jnp.bfloat16)


def attend(order, start, lengths, queries, own_latent, latents, first, rows):
    _, heads, width = queries.shape
    slots, block, _ = latents.shape
    own_latent = own_latent.reshape(own_latent.shape[0], 1, width)
    return pl.pallas_call(
        attend_kernel,
        grid_spec=pltpu.PrefetchScalarGridSpec(
            num_scalar_prefetch=3,
            grid=(rows,),
            in_specs=[
                pl.BlockSpec((1, heads, width), lambda i, *_: (i + first, 0, 0)),
                pl.BlockSpec((1, 1, width), lambda i, *_: (i + first, 0, 0)),
                pl.BlockSpec((slots, block, width), lambda i, *_: (0, 0, 0)),
            ],
            out_specs=pl.BlockSpec((1, heads, KV), lambda i, *_: (i, 0, 0)),
        ),
        out_shape=jax.ShapeDtypeStruct((rows, heads, KV), jnp.bfloat16),
        compiler_params=pltpu.CompilerParams(vmem_limit_bytes=VMEM_LIMIT),
        cost_estimate=pl.CostEstimate(
            flops=2 * slots * heads * block * width,
            bytes_accessed=2 * (rows * heads * (width + KV) + slots * block * width),
            transcendentals=slots * heads * block,
        ),
        name="attend",
    )(order, start[first : first + rows + 1], lengths, queries, own_latent, latents)


def dense_gates(experts, gates, expert_count):
    named = experts[:, :, None] == jnp.arange(expert_count)[None, None, :]
    return jnp.sum(jnp.where(named, gates[:, :, None], 0), axis=1)


def per_device(
    prefill_tokens,
    prefill_experts,
    prefill_gates,
    decode_rows,
    decode_experts,
    decode_gates,
    w_gate_up,
    w_down,
    queries,
    own_latent,
    latents,
    span_owner,
    span_request,
    span_length,
):
    devices = lax.axis_size(AXIS)
    chips = devices // 2
    half = chips // 2
    gate_up = w_gate_up[0]
    down_proj = w_down[0]
    prefill_count = prefill_tokens.shape[0]
    decode_count = decode_rows.shape[0]
    row_count = prefill_count + decode_count
    split = prefill_count

    ring = list(range(0, chips, 2)) + list(range(1, chips, 2))[::-1]
    place_of = np.zeros(chips, np.int32)
    for i, chip in enumerate(ring):
        place_of[chip] = i
    ahead = [
        (2 * ring[i] + c, 2 * ring[(i + 1) % chips] + c) for i in range(chips) for c in range(2)
    ]
    back = [(b, a) for a, b in ahead]
    across = [(i, i ^ 1) for i in range(devices)]
    me = lax.axis_index(AXIS)
    neighbours = np.zeros((devices, chips), np.int32)
    for device in range(devices):
        for shift in range(chips):
            chip = ring[(place_of[device // 2] + shift) % chips]
            neighbours[device, shift] = 2 * chip + device % 2

    span_count = span_owner.shape[0]
    block_rows = latents.shape[1]
    slots = devices * CAPC
    numbered = jnp.arange(span_count)
    earlier = (span_owner[None, :] == span_owner[:, None]) & (numbered[None, :] < numbered[:, None])
    span_rank = jnp.sum(earlier, axis=1)
    slot_of = span_owner * CAPC + span_rank
    placed = slot_of[None, :] == jnp.arange(slots)[:, None]
    source = jnp.sum(jnp.where(placed, numbered[None, :], 0), axis=1).astype(jnp.int32)
    codes = span_request * (block_rows + 1) + span_length
    slot_codes = jnp.sum(jnp.where(placed, codes[None, :], 0), axis=1).astype(jnp.int32)

    gates = jnp.concatenate(
        [
            dense_gates(prefill_experts, prefill_gates, chips),
            dense_gates(decode_experts, decode_gates, chips),
        ],
        axis=0,
    )
    small = jnp.concatenate(
        [jnp.repeat(gates.T, 2, axis=0), slot_codes.reshape(devices, CAPC)], axis=1
    ).astype(jnp.int32)
    small = lax.all_to_all(small, AXIS, split_axis=0, concat_axis=0, tiled=True)
    shipped = ship_blocks(latents, source)

    own = [prefill_tokens, decode_rows]
    sizes = [prefill_count, decode_count]
    front = {1: [lax.ppermute(c, AXIS, ahead) for c in own]}
    rear = {1: [lax.ppermute(c, AXIS, back) for c in own]}
    rear[1][1], shipped, small = lax.optimization_barrier((rear[1][1], shipped, small))
    at_shift = lax.dynamic_index_in_dim(jnp.asarray(neighbours), me, 0, keepdims=False)
    picked = at_shift[:, None] == jnp.arange(devices)[None, :]
    shift_gates = jnp.sum(jnp.where(picked[:, :, None], small[None, :, :row_count], 0), axis=1)
    shift_gates = shift_gates.astype(jnp.float32) / gate_unit
    slot_codes = small[:, row_count:].reshape(-1)
    slot_length = slot_codes % (block_rows + 1)
    slot_request = slot_codes // (block_rows + 1)

    for s in range(2, half):
        front[s] = [lax.ppermute(c, AXIS, ahead) for c in front[s - 1]]
        rear[s] = [lax.ppermute(c, AXIS, back) for c in rear[s - 1]]

    def work(s, mine):
        other = [lax.ppermute(c, AXIS, across) for c in mine]
        return mlp(mine, other, gate_up, down_proj)

    front[half] = [lax.ppermute(front[half - 1][0], AXIS, ahead)]
    rear[half] = [lax.ppermute(rear[half - 1][1], AXIS, back)]
    front, rear, shipped, shift_gates = lax.optimization_barrier(
        (front, rear, shipped, shift_gates)
    )
    block_latents = lax.all_to_all(shipped, AXIS, split_axis=0, concat_axis=0, tiled=True)
    results = {}
    for s in range(half, 0, -1):
        results[s] = work(s, front[s] + rear[s] + (own if s == 1 else []))
    parts = {s: (part, lax.ppermute(rest, AXIS, across)) for s, (part, rest) in results.items()}

    def contribution(s, k, flow):
        part, from_other = parts[max(s, 1)]
        size = sizes[flow]
        lo = flow * split
        if s == half:
            lo = k * split
        elif s == 0:
            lo = lo + 2 * row_count
        else:
            lo = lo + k * row_count
        both = part[lo : lo + size].astype(jnp.float32) + from_other[lo : lo + size].astype(
            jnp.float32
        )
        weight = shift_gates[((-s, s)[k] + chips) % chips, flow * split : flow * split + size]
        return (weight[:, None] * both).astype(jnp.bfloat16)

    key = jnp.where(slot_length > 0, slot_request, decode_count)
    index = jnp.arange(slots)
    before = (key[None, :] < key[:, None]) | (
        (key[None, :] == key[:, None]) & (index[None, :] < index[:, None])
    )
    position = jnp.sum(before, axis=1)
    order = jnp.sum(
        jnp.where(position[None, :] == index[:, None], index[None, :], 0), axis=1
    ).astype(jnp.int32)
    start = jnp.sum(key[None, :] < jnp.arange(decode_count + 1)[:, None], axis=1).astype(jnp.int32)
    first_rows = decode_count // 2

    sums = [{"up": contribution(half, 0, 0)}, {"down": contribution(half, 1, 1)}]
    terms = {
        (s, flow): {"up": contribution(s, 1, flow), "down": contribution(s, 0, flow)}
        for s in range(1, half)
        for flow in range(2)
    }
    last = [contribution(0, 0, flow) for flow in range(2)]
    course = {"up": ahead, "down": back}

    def add(a, b):
        return (a.astype(jnp.float32) + b.astype(jnp.float32)).astype(jnp.bfloat16)

    for s in range(half - 1, -1, -1):
        for flow in range(2):
            moved = {
                way: lax.ppermute(value, AXIS, course[way]) for way, value in sums[flow].items()
            }
            if s == half - 1:
                moved, terms, last, block_latents = lax.optimization_barrier(
                    (moved, terms, last, block_latents)
                )
            else:
                moved = lax.optimization_barrier(moved)
            if s == 0:
                sums[flow] = moved
                continue
            added = {
                way: add(moved[way], term) if way in moved else term
                for way, term in terms[(s, flow)].items()
            }
            if s == 1 and flow == 0:
                early = attend(
                    order, start, slot_length, queries, own_latent, block_latents, 0, first_rows
                )
            if s == 1 and flow == 1:
                added, early = lax.optimization_barrier((added, early))
                late = attend(
                    order,
                    start,
                    slot_length,
                    queries,
                    own_latent,
                    block_latents,
                    first_rows,
                    decode_count - first_rows,
                )
                context = jnp.concatenate([early, late], axis=0)
            sums[flow] = lax.optimization_barrier(added)

    def finish(flow):
        total = sums[flow]["up"].astype(jnp.float32) + sums[flow]["down"].astype(jnp.float32)
        return (total + last[flow].astype(jnp.float32)).astype(jnp.bfloat16)

    return (finish(0), finish(1), context)


def solution(mesh):
    rows = P(("groups", "expert"), None)
    blocks = P(("groups", "expert"), None, None)
    line = P(("groups", "expert"))
    weights = P("expert", None, None)
    return jax.shard_map(
        per_device,
        mesh=mesh,
        in_specs=(rows,) * 6 + (weights, weights, blocks, rows, blocks, line, line, line),
        out_specs=(rows, rows, blocks),
        check_vma=False,
    )
```
